128 devices in a mesh: group: 4 (over x), head: 32 (over z, y, core).
Axes of the slice: x: 4, y: 4, z: 4, core: 2. Of those that a mesh axis runs over, the one named last changes fastest.
Arguments:
- queries: bfloat16 [256, 8192], P(('group', 'head')), may hold values from -124 to 124
- prefix_keys: bfloat16 [16384, 1024], P('head'), may hold values from -4.5 to 4.5
- prefix_values: bfloat16 [16384, 1024], P('head'), may hold values from -6 to 6
- suffix_keys: bfloat16 [256, 64, 1024], P('group', 'head'), may hold values from -6 to 6
- suffix_values: bfloat16 [256, 64, 1024], P('group', 'head'), may hold values from -6 to 6
- suffix_lengths: int32 [256], P('group'), may hold values from 1 to 64
- hidden_in: bfloat16 [256, 8192], P(('group', 'head')), may hold values from -0.29882812 to 0.29882812
- w_out: bfloat16 [8192, 8192], P('head'), may hold values from -0.0625 to 0.0625
- norm_gain: bfloat16 [8192], replicated, may hold values from 0.099609375 to 1.8984375
- expert_ids: int32 [256, 2], P(('group', 'head')), may hold values from 0 to 3, all different within a row; in each aligned block of 2 rows (0 to 1, 2 to 3, ...) at most 2 rows name the same one
- expert_weights: float32 [256, 2], P(('group', 'head')), may hold values from 0.2 to 1
- w_gate: bfloat16 [4, 8192, 12288], P('group', None, 'head'), may hold values from -0.0625 to 0.0625
- w_up: bfloat16 [4, 8192, 12288], P('group', None, 'head'), may hold values from -0.0625 to 0.0625
- w_down: bfloat16 [4, 12288, 8192], P('group', 'head'), may hold values from -0.0546875 to 0.0546875
Outputs:
- mixed: bfloat16 [256, 8192], P(('group', 'head'))
The draws below stay inside these ranges and needn't reach their ends.
Inputs may be any that keep to these rules, and one draw needn't show every extreme that they name: `expert_ids`: each row names 2 different experts; the 2 rows of one device name any one expert 2 times at most.
All inputs are finite; a program needn't handle non-finite values.
Results may differ from the reference program's by a relative error of at most 0.027.
Values may be sent and summed in bfloat16 or wider, within the bound.
No kernel may reach another device: no remote copies, remote signals or barrier semaphores. Data moves between devices by JAX's collectives and lax.ppermute only.
A program may use at most 320 MiB of HBM per device.

```python
import math
import jax
import jax.numpy as jnp
import numpy as np
from jax import lax

D = 8192
HEADS = 64
KV = 8
HD = 128
FF = 12288
TOP = 2
ROW_DEV = 2
CAP = 2
EXPERTS = 4
ROWS = 256
PREFIX = 16384
SUFFIX = 64
N_HEAD = 32


def shared_keys(key):
    base = jax.random.fold_in(key, 11)
    keys_all = jnp.clip(jax.random.normal(base, (PREFIX, KV * HD), jnp.float32), -4.5, 4.5)
    ordering = jax.random.permutation(jax.random.fold_in(key, 12), PREFIX // 2)
    spots = 2 * ordering[:8]
    twins = keys_all[spots + 1]
    keys_all = keys_all.at[spots + 1].set(twins)
    planted = 2 * ordering[8]
    mixed = keys_all[planted, :HD]
    keys_all = keys_all.at[planted, :HD].set(mixed)
    return keys_all


def draw_prefix_keys(key, part):
    keys_all = shared_keys(key)
    return keys_all.astype(jnp.bfloat16)


def draw_queries(key, part):
    key = jax.random.fold_in(key, 3)
    drawn = jnp.clip(jax.random.normal(key, (ROWS, HEADS * HD), jnp.float32), -4.5, 4.5)
    return drawn.astype(jnp.bfloat16)


def draw_suffix_lengths(key, part):
    key = jax.random.fold_in(key, 5)
    lengths = jax.random.randint(key, (ROWS,), 1, SUFFIX + 1)
    longest = jax.random.randint(jax.random.fold_in(key, 6), (), 0, ROWS)
    lengths = lengths.at[longest].set(SUFFIX)
    return lengths.astype(jnp.int32)


def level_of(stream_key, dims, shards, smallest, largest):
    loudness = 1.0
    for position, parts in shards:
        draws = jax.random.uniform(jax.random.fold_in(jax.random.fold_in(stream_key, 6), position), (parts,), jnp.float32, smallest / len(shards), largest / len(shards))
        loudness = loudness * jnp.repeat(jnp.exp(draws), dims[position] // parts).reshape((-1,) + (1,) * (len(dims) - 1 - position))
    return loudness


def deal_out(own_key, own, number, rows, count, top, limit, slope):
    order = jax.random.permutation(own_key, count)
    crowded, common = shares(count, rows * top, limit, slope, True), shares(count, rows * top, limit, slope, False)
    places = jnp.arange(count)

    def named(sizes, turn):
        used = int((sizes > 0).sum())
        fixed = max(1, used // 4)
        shifted = fixed + (places - fixed + turn * (used - fixed)) % max(1, count - fixed)
        return jnp.zeros((count,), jnp.int32).at[order[jnp.where(places < fixed, places, shifted)]].set(jnp.asarray(sizes, jnp.int32))

    sizes = jnp.where(number % 4 == 0, named(crowded, number // 4), named(common, number - number // 4 - 1))
    mixed = jax.random.permutation(jax.random.fold_in(own, 3), count)
    donor, taker = mixed[0:count // 2 * 2:2], mixed[1:count // 2 * 2:2]
    slack = jnp.minimum(sizes[donor] - 1, limit - sizes[taker]) // 2
    slack = jnp.where((donor == order[0]) | (taker == order[0]) | (sizes[taker] == 0), 0, jnp.maximum(slack, 0))
    shifted = jax.random.randint(jax.random.fold_in(own, 4), (count // 2,), 0, 1 << 20) % (slack + 1)
    sizes = sizes.at[donor].add(-shifted).at[taker].add(shifted)
    items = jnp.searchsorted(jnp.cumsum(sizes), jnp.arange(rows * top), side="right").astype(jnp.int32)
    listing = items.reshape(top, rows).T
    listing = listing[jax.random.permutation(jax.random.fold_in(own, 1), rows)]
    turn = jax.random.randint(jax.random.fold_in(own, 2), (rows, 1), 0, top)
    return jnp.take_along_axis(listing, (jnp.arange(top)[None, :] + turn) % top, axis=1)


def shares(number_of, total, limit, lean, full):
    weights = [(1 << 20) // math.isqrt(standing ** lean) + 1 for standing in range(1, number_of + 1)]
    largest = limit if full else min(limit, max(-(-total // number_of), total * weights[0] // sum(weights)))
    least = 1 if total - largest >= number_of - 1 else 0
    counts, surplus = [largest] + [least] * (number_of - 1), total - largest - least * (number_of - 1)
    while surplus > 0:
        candidates = [i for i in range(1, number_of) if counts[i] < largest] or [i for i in range(1, number_of) if counts[i] < limit]
        whole, remaining = sum([weights[i] for i in candidates]), surplus
        for i in candidates:
            addition = min(limit - counts[i], max(1, remaining * weights[i] // whole), surplus)
            counts[i] = counts[i] + addition
            surplus = surplus - addition
    return np.array(counts)


def bell_draw(own_key, shape, deviation, most, cuts=(), held_as=jnp.bfloat16):
    entries = jax.random.normal(own_key, shape, jnp.float32) * deviation
    if len(cuts) > 0:
        entries = level_of(own_key, shape, cuts, -0.22, 0.18) * entries
    return jnp.clip(entries, min=-most, max=most).astype(held_as)


def setup_inputs(seed: int = 0) -> dict:
    keys = jax.random.split(jax.random.key(seed), 15)
    queries = draw_queries(jax.random.fold_in(keys[14], 71), 0)
    prefix_keys = draw_prefix_keys(jax.random.fold_in(keys[14], 71), 0)
    prefix_values = bell_draw(keys[2], (PREFIX, KV * HD), 1.0, 6.0, ((0, 32),))
    suffix_keys = bell_draw(keys[3], (ROWS, SUFFIX, KV * HD), 1.0, 6.0, ((0, 4), (1, 32)))
    suffix_values = bell_draw(keys[4], (ROWS, SUFFIX, KV * HD), 1.0, 6.0, ((0, 4), (1, 32)))
    suffix_lengths = draw_suffix_lengths(jax.random.fold_in(keys[14], 71), 0)
    hidden_in = bell_draw(keys[6], (ROWS, D), 0.05, 0.29882812, ((0, 128),))
    w_out = bell_draw(keys[7], (HEADS * HD, D), (HEADS * HD) ** -0.5, 0.0625, ((0, 32),))
    norm_gain = jnp.clip(1.0 + 0.18 * jax.random.normal(keys[8], (D,), jnp.float32), 0.099609375, 1.8984375).astype(jnp.bfloat16)
    expert_ids_keys = jax.random.split(jax.random.fold_in(keys[9], 1), ROWS // ROW_DEV)
    expert_ids_turns = jax.random.permutation(jax.random.fold_in(keys[9], 3), ROWS // ROW_DEV)
    expert_ids = jax.vmap(lambda own, number: deal_out(jax.random.fold_in(keys[9], 2), own, number, ROW_DEV, EXPERTS, TOP, CAP, 2))(expert_ids_keys, expert_ids_turns).reshape((ROWS, TOP))
    expert_weights = jnp.clip(0.2 + 0.8 * jax.random.uniform(keys[10], (ROWS, TOP), jnp.float32) ** level_of(keys[10], (ROWS, TOP), ((0, 128),), -0.2, 0.2), 0.2, 1.0)
    w_gate = bell_draw(keys[11], (EXPERTS, D, FF), D ** -0.5, 0.0625, ((0, 4), (2, 32)))
    w_up = bell_draw(keys[12], (EXPERTS, D, FF), D ** -0.5, 0.0625, ((0, 4), (2, 32)))
    w_down = bell_draw(keys[13], (EXPERTS, FF, D), FF ** -0.5, 0.0546875, ((0, 4), (1, 32)))
    return {"queries": queries, "prefix_keys": prefix_keys, "prefix_values": prefix_values, "suffix_keys": suffix_keys, "suffix_values": suffix_values, "suffix_lengths": suffix_lengths, "hidden_in": hidden_in, "w_out": w_out, "norm_gain": norm_gain, "expert_ids": expert_ids, "expert_weights": expert_weights, "w_gate": w_gate, "w_up": w_up, "w_down": w_down}


NEG = -1e+30
EPS = 1e-05

def attend_block(query_blk, suffix_key_blk, suffix_val_blk, length_blk, prefix_keys, prefix_values):
    count_rows = query_blk.shape[0]
    per_group = HEADS // KV
    scaling = 1.0 / HD ** 0.5
    query_grid = query_blk.astype(jnp.float32).reshape(count_rows, KV, per_group, HD)
    prefix_k = prefix_keys.astype(jnp.float32).reshape(PREFIX, KV, HD)
    prefix_v = prefix_values.astype(jnp.float32).reshape(PREFIX, KV, HD)
    suffix_k = suffix_key_blk.astype(jnp.float32).reshape(count_rows, SUFFIX, KV, HD)
    suffix_v = suffix_val_blk.astype(jnp.float32).reshape(count_rows, SUFFIX, KV, HD)
    prefix_scores = jnp.einsum('rkgd,pkd->rkgp', query_grid, prefix_k) * scaling
    suffix_scores = jnp.einsum('rkgd,rskd->rkgs', query_grid, suffix_k) * scaling
    live_mask = jnp.arange(SUFFIX, dtype=jnp.int32)[None, :] < length_blk[:, None]
    suffix_scores = jnp.where(live_mask[:, None, None, :], suffix_scores, NEG)
    highest = jnp.maximum(lax.optimization_barrier(jnp.max(prefix_scores, axis=-1)), lax.optimization_barrier(jnp.max(suffix_scores, axis=-1)))
    prefix_prob = jnp.exp(prefix_scores - highest[..., None])
    suffix_prob = jnp.exp(suffix_scores - highest[..., None])
    totals = lax.optimization_barrier(jnp.sum(prefix_prob, axis=-1)) + lax.optimization_barrier(jnp.sum(suffix_prob, axis=-1))
    weighted = jnp.einsum('rkgp,pkd->rkgd', prefix_prob.astype(jnp.bfloat16).astype(jnp.float32), prefix_v)
    weighted = weighted + jnp.einsum('rkgs,rskd->rkgd', suffix_prob.astype(jnp.bfloat16).astype(jnp.float32), suffix_v)
    attended = weighted / totals[..., None]
    return attended.reshape(count_rows, HEADS * HD).astype(jnp.bfloat16)

def blockwise_down(inner, down_matrix):
    block_width = FF // N_HEAD
    count_rows = inner.shape[0]
    inner_blocks = jnp.swapaxes(inner.reshape(count_rows, N_HEAD, block_width), 0, 1)
    down_blocks = down_matrix.reshape(N_HEAD, block_width, D)

    def add_block(carry, pieces):
        inner_blk, down_blk = pieces
        partial_sum = jnp.dot(inner_blk, down_blk, preferred_element_type=jnp.float32)
        rounded = lax.optimization_barrier(partial_sum.astype(jnp.bfloat16))
        return (carry + rounded.astype(jnp.float32), None)
    start = jnp.zeros((count_rows, D), jnp.float32)
    total, unused = lax.scan(add_block, start, (inner_blocks, down_blocks))
    return total

def reference(queries, prefix_keys, prefix_values, suffix_keys, suffix_values, suffix_lengths, hidden_in, w_out, norm_gain, expert_ids, expert_weights, w_gate, w_up, w_down):
    blocks = 16
    per_block = ROWS // blocks

    def one_block(pieces):
        query_blk, key_blk, val_blk, length_blk = pieces
        return attend_block(query_blk, key_blk, val_blk, length_blk, prefix_keys, prefix_values)
    attended = lax.map(one_block, (queries.reshape(blocks, per_block, HEADS * HD), suffix_keys.reshape(blocks, per_block, SUFFIX, KV * HD), suffix_values.reshape(blocks, per_block, SUFFIX, KV * HD), suffix_lengths.reshape(blocks, per_block)))
    attended = attended.reshape(ROWS, HEADS * HD)
    residual = hidden_in.astype(jnp.float32) + jnp.dot(attended, w_out, preferred_element_type=jnp.float32)
    mean_square = lax.optimization_barrier(jnp.mean(residual * residual, axis=-1, keepdims=True))
    normed = (residual * lax.rsqrt(mean_square + EPS) * norm_gain.astype(jnp.float32)).astype(jnp.bfloat16)
    bound = ROWS * CAP // ROW_DEV
    mixture = jnp.zeros((ROWS, D), jnp.float32)
    for expert in range(EXPERTS):
        match = expert_ids == expert
        chosen = jnp.any(match, axis=1)
        weight_row = lax.optimization_barrier(jnp.sum(jnp.where(match, expert_weights, 0.0), axis=1))
        order = jnp.argsort(jnp.where(chosen, 0, 1).astype(jnp.int32), stable=True)[:bound].astype(jnp.int32)
        picked = normed[order]
        gate_val = jnp.dot(picked, w_gate[expert], preferred_element_type=jnp.float32)
        up_val = jnp.dot(picked, w_up[expert], preferred_element_type=jnp.float32)
        inner = (jax.nn.silu(gate_val) * up_val).astype(jnp.bfloat16)
        expert_out = blockwise_down(inner, w_down[expert])
        factor = jnp.where(chosen[order], weight_row[order], 0.0)
        mixture = mixture.at[order].add(factor[:, None] * expert_out)
    return (residual + mixture).astype(jnp.bfloat16)
```

```python
import functools

import jax
import jax.numpy as jnp
from jax import lax
from jax.experimental import pallas as pl
from jax.experimental.pallas import tpu as pltpu
from jax.sharding import Mesh, PartitionSpec as P

HEADS = 64
KV = 8
HD = 128
D = 8192
HALF = D // 2
EPS = 1e-05
NEG = -1e30
LOG2E = 1.4426950408889634
SCALE = LOG2E / HD**0.5
BF = jnp.bfloat16
F32 = jnp.float32
ALL = ("x", "z", "y", "c")
PLANE = ("z", "y", "c")
SWAP = [(0, 1), (1, 0)]
MB = 1 << 20


def dot(a, b):
    return jnp.dot(a, b, preferred_element_type=F32)


def dot_t(a, b):
    return lax.dot_general(a, b, (((1,), (1,)), ((), ())), preferred_element_type=F32)


def attend_kernel(q_ref, ka_ref, kb_ref, va_ref, vb_ref, ska_ref, skb_ref, sva_ref, svb_ref, left_ref, out_ref):
    rows = 64
    q = jnp.concatenate([q_ref[:, g * HD : (g + 1) * HD] for g in range(4)], axis=0)
    row = lax.broadcasted_iota(jnp.int32, (4 * rows, 2 * rows), 0) % rows
    col = lax.broadcasted_iota(jnp.int32, (4 * rows, 2 * rows), 1)
    own_row = row == col // 2
    spot = col % 2
    left = left_ref[...]
    scores = [
        dot_t(q, ka_ref[...]) * SCALE,
        dot_t(q, kb_ref[...]) * SCALE,
        jnp.where(own_row & (spot < left[:, 0:1]), dot_t(q, ska_ref[...]) * SCALE, NEG),
        jnp.where(own_row & (spot < left[:, 1:2]), dot_t(q, skb_ref[...]) * SCALE, NEG),
    ]
    tops = [jnp.max(s, axis=1, keepdims=True) for s in scores]
    top = jnp.maximum(jnp.maximum(tops[0], tops[1]), jnp.maximum(tops[2], tops[3]))
    top = top.astype(BF).astype(F32)
    total = jnp.zeros((4 * rows, 1), F32)
    acc = jnp.zeros((4 * rows, HD), F32)
    for s, v in zip(scores, (va_ref, vb_ref, sva_ref, svb_ref)):
        prob = jnp.exp2(s - top)
        total = total + jnp.sum(prob, axis=1, keepdims=True)
        acc = acc + dot(prob.astype(BF), v[...])
    eye = lax.broadcasted_iota(jnp.int32, (4 * rows, 4 * rows), 0) == lax.broadcasted_iota(
        jnp.int32, (4 * rows, 4 * rows), 1
    )
    top_row = jnp.sum(jnp.where(eye, top, 0.0), axis=0, keepdims=True)
    total_row = jnp.sum(jnp.where(eye, total, 0.0), axis=0, keepdims=True)
    total_high = total_row.astype(BF).astype(F32)
    total_low = total_row - total_high
    line = lax.broadcasted_iota(jnp.int32, (16, 4 * rows), 0)
    for k in range(2):
        for j in range(2):
            g = 2 * k + j
            out_ref[k, 0:rows, j * HD : (j + 1) * HD] = acc[g * rows : (g + 1) * rows].astype(BF)
        part = slice(k * 2 * rows, (k + 1) * 2 * rows)
        high = jnp.concatenate([top_row[:, part], total_high[:, part]], axis=1)
        low = jnp.concatenate([top_row[:, part], total_low[:, part]], axis=1)
        tail = jnp.where(line == 0, high, jnp.where(line == 1, low, 0.0))
        out_ref[k, rows : rows + 16, :] = tail.astype(BF)


def attend(q, ka, kb, va, vb, sa, sb, left):
    full = lambda n: pl.BlockSpec((n, HD), lambda i: (0, i))
    second = lambda n: pl.BlockSpec((n, HD), lambda i: (0, i + KV))
    return pl.pallas_call(
        attend_kernel,
        grid=(KV,),
        in_specs=[
            pl.BlockSpec((64, 4 * HD), lambda i: (0, i)),
            full(512),
            full(512),
            full(512),
            full(512),
            full(128),
            full(128),
            second(128),
            second(128),
            pl.BlockSpec((256, 2), lambda i: (0, 0)),
        ],
        out_specs=pl.BlockSpec((2, 80, 2 * HD), lambda i: (i, 0, 0)),
        out_shape=jax.ShapeDtypeStruct((16, 80, 2 * HD), BF),
        compiler_params=pltpu.CompilerParams(vmem_limit_bytes=32 * MB),
        cost_estimate=pl.CostEstimate(flops=1400000000, bytes_accessed=6 * MB, transcendentals=2700000),
    )(q, ka, kb, va, vb, sa, sb, sa, sb, left)


def project_kernel(c_ref, got_ref, w_ref, mine_ref, other_ref, att_ref):
    rows = 64
    n = pl.program_id(0)

    @pl.when(n == 0)
    def _():
        tops = [got_ref[s, rows : rows + 1, 0 : 2 * rows].astype(F32) for s in range(16)]
        sums = [
            got_ref[s, rows : rows + 1, 2 * rows :].astype(F32)
            + got_ref[s, rows + 1 : rows + 2, 2 * rows :].astype(F32)
            for s in range(16)
        ]
        top = functools.reduce(jnp.maximum, tops)
        factors = [jnp.exp2(t - top) for t in tops]
        total = functools.reduce(jnp.add, [f * s for f, s in zip(factors, sums)])
        lane = lax.broadcasted_iota(jnp.int32, (rows, 2 * rows), 1)
        line = lax.broadcasted_iota(jnp.int32, (rows, 2 * rows), 0)
        for j in range(2):
            here = lane == line + j * rows
            acc = jnp.zeros((rows, HD), F32)
            for s in range(16):
                share = jnp.sum(jnp.where(here, factors[s] / total, 0.0), axis=1, keepdims=True)
                acc = acc + got_ref[s, 0:rows, j * HD : (j + 1) * HD].astype(F32) * share
            att_ref[:, j * HD : (j + 1) * HD] = acc.astype(BF)

    value = dot(att_ref[...], w_ref[...]).astype(BF)

    @pl.when(n < 4)
    def _():
        other_ref[...] = value

    @pl.when(n >= 4)
    def _():
        mine_ref[...] = value


def project(core, got, w_out):
    block = D // 8
    return pl.pallas_call(
        project_kernel,
        grid_spec=pltpu.PrefetchScalarGridSpec(
            num_scalar_prefetch=1,
            grid=(8,),
            in_specs=[
                pl.BlockSpec((16, 80, 256), lambda n, c: (0, 0, 0)),
                pl.BlockSpec((256, block), lambda n, c: (0, (n + 4 * (1 - c[0])) % 8)),
            ],
            out_specs=[
                pl.BlockSpec((64, block), lambda n, c: (0, jnp.maximum(n - 4, 0))),
                pl.BlockSpec((64, block), lambda n, c: (0, jnp.minimum(n, 3))),
            ],
            scratch_shapes=[pltpu.VMEM((64, 256), BF)],
        ),
        out_shape=[jax.ShapeDtypeStruct((64, HALF), BF)] * 2,
        compiler_params=pltpu.CompilerParams(vmem_limit_bytes=32 * MB),
        cost_estimate=pl.CostEstimate(flops=270000000, bytes_accessed=6 * MB, transcendentals=0),
    )(core, got, w_out)


def first_kernel(c_ref, x_ref, wg_ref, wu_ref, g_ref, u_ref):
    @pl.when(pl.program_id(0) == 0)
    def _():
        g_ref[...] = jnp.zeros_like(g_ref)
        u_ref[...] = jnp.zeros_like(u_ref)

    x = x_ref[...]
    g_ref[...] += dot(x, wg_ref[...])
    u_ref[...] += dot(x, wu_ref[...])


def expert_first(core, x, w_gate, w_up):
    rows, units = x.shape[0], w_gate.shape[1]
    block = 1024
    return pl.pallas_call(
        first_kernel,
        grid_spec=pltpu.PrefetchScalarGridSpec(
            num_scalar_prefetch=1,
            grid=(4,),
            in_specs=[
                pl.BlockSpec((rows, block), lambda n, c: (0, n)),
                pl.BlockSpec((block, units), lambda n, c: (n + 4 * c[0], 0)),
                pl.BlockSpec((block, units), lambda n, c: (n + 4 * c[0], 0)),
            ],
            out_specs=[pl.BlockSpec((rows, units), lambda n, c: (0, 0))] * 2,
        ),
        out_shape=[jax.ShapeDtypeStruct((rows, units), F32)] * 2,
        compiler_params=pltpu.CompilerParams(vmem_limit_bytes=32 * MB),
        cost_estimate=pl.CostEstimate(flops=1600000000, bytes_accessed=9 * MB, transcendentals=0),
    )(core, x, w_gate, w_up)


def second_kernel(c_ref, x_ref, wg_ref, wu_ref, g0_ref, u0_ref, wd_ref, inner_ref, out_ref, g_ref, u_ref):
    n = pl.program_id(0)

    @pl.when(n == 0)
    def _():
        g_ref[...] = g0_ref[...]
        u_ref[...] = u0_ref[...]

    @pl.when(n < 4)
    def _():
        x = x_ref[...]
        g_ref[...] += dot(x, wg_ref[...])
        u_ref[...] += dot(x, wu_ref[...])

    @pl.when(n == 3)
    def _():
        g = g_ref[...]
        inner_ref[...] = (g / (1.0 + jnp.exp(-g)) * u_ref[...]).astype(BF)

    @pl.when(n >= 4)
    def _():
        out_ref[...] = dot(inner_ref[...], wd_ref[...]).astype(BF)


def expert_second(core, x, w_gate, w_up, gate, up, w_down):
    rows, units = x.shape[0], w_gate.shape[1]
    block = 1024
    early = lambda n: jnp.minimum(n, 3)
    late = lambda n: jnp.maximum(n - 4, 0)
    whole = pl.BlockSpec((rows, units), lambda n, c: (0, 0))
    return pl.pallas_call(
        second_kernel,
        grid_spec=pltpu.PrefetchScalarGridSpec(
            num_scalar_prefetch=1,
            grid=(8,),
            in_specs=[
                pl.BlockSpec((rows, block), lambda n, c: (0, early(n))),
                pl.BlockSpec((block, units), lambda n, c: (early(n) + 4 * (1 - c[0]), 0)),
                pl.BlockSpec((block, units), lambda n, c: (early(n) + 4 * (1 - c[0]), 0)),
                whole,
                whole,
                pl.BlockSpec((units, block), lambda n, c: (0, late(n) + 4 * (1 - c[0]))),
            ],
            out_specs=[whole, pl.BlockSpec((rows, block), lambda n, c: (0, late(n)))],
            scratch_shapes=[pltpu.VMEM((rows, units), F32), pltpu.VMEM((rows, units), F32)],
        ),
        out_shape=[
            jax.ShapeDtypeStruct((rows, units), BF),
            jax.ShapeDtypeStruct((rows, HALF), BF),
        ],
        compiler_params=pltpu.CompilerParams(vmem_limit_bytes=32 * MB),
        cost_estimate=pl.CostEstimate(flops=2400000000, bytes_accessed=15 * MB, transcendentals=0),
    )(core, x, w_gate, w_up, gate, up, w_down)


def third_kernel(c_ref, inner_ref, wd_ref, out_ref):
    out_ref[...] = dot(inner_ref[...], wd_ref[...]).astype(BF)


def expert_third(core, inner, w_down):
    rows, units = inner.shape
    block = 1024
    return pl.pallas_call(
        third_kernel,
        grid_spec=pltpu.PrefetchScalarGridSpec(
            num_scalar_prefetch=1,
            grid=(4,),
            in_specs=[
                pl.BlockSpec((rows, units), lambda n, c: (0, 0)),
                pl.BlockSpec((units, block), lambda n, c: (0, n + 4 * c[0])),
            ],
            out_specs=pl.BlockSpec((rows, block), lambda n, c: (0, n)),
        ),
        out_shape=jax.ShapeDtypeStruct((rows, HALF), BF),
        compiler_params=pltpu.CompilerParams(vmem_limit_bytes=32 * MB),
        cost_estimate=pl.CostEstimate(flops=800000000, bytes_accessed=6 * MB, transcendentals=0),
    )(core, inner, w_down)


def local(
    queries,
    prefix_keys,
    prefix_values,
    suffix_keys,
    suffix_values,
    suffix_lengths,
    hidden_in,
    w_out,
    norm_gain,
    expert_ids,
    expert_weights,
    w_gate,
    w_up,
    w_down,
):
    c = lax.axis_index("c")
    chip = lax.axis_index(("z", "y"))
    core = c.astype(jnp.int32).reshape(1)
    suffix = jnp.concatenate([suffix_keys, suffix_values], axis=-1).reshape(128, 2 * KV * HD)
    suffix_b = lax.ppermute(suffix, "c", SWAP)
    keys_b = lax.ppermute(prefix_keys, "c", SWAP)
    values_b = lax.ppermute(prefix_values, "c", SWAP)
    q = queries.reshape(2, 16, 2, 2 * HD).transpose(2, 0, 1, 3).reshape(1, 2, 2, HALF)
    q = jnp.broadcast_to(q, (16, 2, 2, HALF)).reshape(32, 2, HALF)
    q = lax.all_to_all(q, PLANE, split_axis=0, concat_axis=0, tiled=True).reshape(64, HALF)
    first = 4 * chip
    left = jnp.stack([suffix_lengths - (first + 2 * c), suffix_lengths - (first + 2 * (1 - c))], axis=1)
    left = jnp.tile(left.astype(jnp.int32), (4, 1))
    parts = attend(q, prefix_keys, keys_b, prefix_values, values_b, suffix, suffix_b, left)
    parts = lax.all_to_all(parts, ("z", "y"), split_axis=0, concat_axis=0, tiled=True)
    mine, other = project(core, parts, w_out)
    other = lax.ppermute(other, "c", SWAP)
    summed = (mine.astype(F32) + other.astype(F32)).astype(BF).reshape(32, 2, HALF)
    summed = lax.all_to_all(summed, PLANE, split_axis=0, concat_axis=0, tiled=True)
    summed = jnp.sum(summed.reshape(16, 2, 2, HALF).astype(F32), axis=0)
    residual = hidden_in.astype(F32) + jnp.swapaxes(summed, 0, 1).reshape(2, D)
    mean_square = jnp.mean(residual * residual, axis=-1, keepdims=True)
    normed = (residual * lax.rsqrt(mean_square + EPS) * norm_gain.astype(F32)).astype(BF)
    sent = jnp.swapaxes(normed.reshape(2, 2, HALF), 0, 1)[None]
    sent = jnp.broadcast_to(sent, (64, 2, 2, HALF)).reshape(128, 2, HALF)
    rows_a = lax.all_to_all(sent, ALL, split_axis=0, concat_axis=0, tiled=True).reshape(256, HALF)
    rows_b = lax.ppermute(rows_a, "c", SWAP)
    gate, up = expert_first(core, rows_a, w_gate[0], w_up[0])
    inner, other_out = expert_second(core, rows_b, w_gate[0], w_up[0], gate, up, w_down[0])
    other_out = lax.ppermute(other_out, "c", SWAP)
    mine_out = expert_third(core, inner, w_down[0])
    out = (mine_out.astype(F32) + other_out.astype(F32)).astype(BF).reshape(128, 2, HALF)
    out = lax.all_to_all(out, ALL, split_axis=0, concat_axis=0, tiled=True)
    out = jnp.sum(out.reshape(4, 16, 2, 2, HALF).astype(F32), axis=1)
    match = expert_ids[:, :, None] == jnp.arange(4, dtype=jnp.int32)[None, None, :]
    weights = jnp.sum(jnp.where(match, expert_weights[:, :, None], 0.0), axis=1)
    mixture = jnp.sum(out * weights.T[:, None, :, None], axis=0)
    mixture = jnp.swapaxes(mixture, 0, 1).reshape(2, D)
    return (residual + mixture).astype(BF)


def solution(mesh):
    grid = Mesh(mesh.devices.reshape(4, 4, 4, 2), ALL)
    placed = (
        P(ALL, None),
        P(PLANE, None),
        P(PLANE, None),
        P("x", PLANE, None),
        P("x", PLANE, None),
        P("x"),
        P(ALL, None),
        P(PLANE, None),
        P(),
        P(ALL, None),
        P(ALL, None),
        P("x", None, PLANE),
        P("x", None, PLANE),
        P("x", PLANE, None),
    )
    return jax.shard_map(
        local, mesh=grid, in_specs=placed, out_specs=P(ALL, None), check_vma=False
    )
```

```python
import functools

import jax
import jax.numpy as jnp
from jax import lax
from jax.experimental import pallas as pl
from jax.experimental.pallas import tpu as pltpu
from jax.sharding import Mesh, PartitionSpec as P

HEADS = 64
KV = 8
HD = 128
D = 8192
HALF = D // 2
EPS = 1e-05
NEG = -1e30
LOG2E = 1.4426950408889634
SCALE = LOG2E / HD**0.5
BF = jnp.bfloat16
F32 = jnp.float32
ALL = ("x", "z", "y", "c")
PLANE = ("z", "y", "c")
SWAP = [(0, 1), (1, 0)]
MB = 1 << 20


def device(x, z, y, c):
    return ((x * 4 + z) * 4 + y) * 2 + c


def wide_groups():
    four = range(4)
    zeros = [[device(x, z, y, 0) for z in four for x in four] for y in four]
    return zeros + [[device(x, z, y, 1) for y in four for x in four] for z in four]


def line_shift(step):
    pairs = []
    for z in range(4):
        for y in range(4):
            pairs.append(((z * 4 + y) * 2, (z * 4 + (y + step) % 4) * 2))
            pairs.append(((z * 4 + y) * 2 + 1, (((z + step) % 4) * 4 + y) * 2 + 1))
    return pairs


def dot(a, b):
    return jnp.dot(a, b, preferred_element_type=F32)


def dot_t(a, b):
    return lax.dot_general(a, b, (((1,), (1,)), ((), ())), preferred_element_type=F32)


def fetch_kernel(*refs):
    sources, targets, sems = refs[1:4], refs[4:7], refs[7]
    copies = []
    for source, target in zip(sources, targets):
        rows = source.shape[0] // 4
        for part in range(4):
            at = pl.ds(part * rows, rows)
            copies.append(pltpu.make_async_copy(source.at[at], target.at[at], sems.at[len(copies)]))
    for copy in copies:
        copy.start()
    for copy in copies:
        copy.wait()


def fetch(after, *arrays):
    return pl.pallas_call(
        fetch_kernel,
        in_specs=[pl.BlockSpec(memory_space=pl.ANY)] * 4,
        out_specs=[pl.BlockSpec(memory_space=pltpu.VMEM)] * 3,
        out_shape=[pltpu.VMEM(a.shape, a.dtype) for a in arrays],
        scratch_shapes=[pltpu.SemaphoreType.DMA((12,))],
        compiler_params=pltpu.CompilerParams(vmem_limit_bytes=4 * MB),
        cost_estimate=pl.CostEstimate(flops=0, bytes_accessed=22 * MB, transcendentals=0),
    )(after, *[in_hbm(a) for a in arrays])


def in_vmem(array):
    return pltpu.with_memory_space_constraint(array, pltpu.VMEM)


def in_hbm(array):
    return pltpu.with_memory_space_constraint(array, pltpu.HBM)


def attend_kernel(q_ref, ka_ref, kb_ref, va_ref, vb_ref, ska_ref, skb_ref, sva_ref, svb_ref, left_ref, out_ref):
    rows = 64
    q = jnp.concatenate([q_ref[:, g * HD : (g + 1) * HD] for g in range(4)], axis=0)
    row = lax.broadcasted_iota(jnp.int32, (4 * rows, 2 * rows), 0) % rows
    col = lax.broadcasted_iota(jnp.int32, (4 * rows, 2 * rows), 1)
    own_row = row == col // 2
    spot = col % 2
    left = left_ref[...]
    scores = [
        dot_t(q, ka_ref[...]) * SCALE,
        dot_t(q, kb_ref[...]) * SCALE,
        jnp.where(own_row & (spot < left[:, 0:1]), dot_t(q, ska_ref[...]) * SCALE, NEG),
        jnp.where(own_row & (spot < left[:, 1:2]), dot_t(q, skb_ref[...]) * SCALE, NEG),
    ]
    tops = [jnp.max(s, axis=1, keepdims=True) for s in scores]
    top = jnp.maximum(jnp.maximum(tops[0], tops[1]), jnp.maximum(tops[2], tops[3]))
    top = top.astype(BF).astype(F32)
    total = jnp.zeros((4 * rows, 1), F32)
    acc = jnp.zeros((4 * rows, HD), F32)
    for s, v in zip(scores, (va_ref, vb_ref, sva_ref, svb_ref)):
        prob = jnp.exp2(s - top)
        total = total + jnp.sum(prob, axis=1, keepdims=True)
        acc = acc + dot(prob.astype(BF), v[...])
    eye = lax.broadcasted_iota(jnp.int32, (4 * rows, 4 * rows), 0) == lax.broadcasted_iota(
        jnp.int32, (4 * rows, 4 * rows), 1
    )
    top_row = jnp.sum(jnp.where(eye, top, 0.0), axis=0, keepdims=True)
    total_row = jnp.sum(jnp.where(eye, total, 0.0), axis=0, keepdims=True)
    total_high = total_row.astype(BF).astype(F32)
    total_low = total_row - total_high
    line = lax.broadcasted_iota(jnp.int32, (16, 4 * rows), 0)
    for k in range(2):
        for j in range(2):
            g = 2 * k + j
            out_ref[k, 0:rows, j * HD : (j + 1) * HD] = acc[g * rows : (g + 1) * rows].astype(BF)
        part = slice(k * 2 * rows, (k + 1) * 2 * rows)
        high = jnp.concatenate([top_row[:, part], total_high[:, part]], axis=1)
        low = jnp.concatenate([top_row[:, part], total_low[:, part]], axis=1)
        tail = jnp.where(line == 0, high, jnp.where(line == 1, low, 0.0))
        out_ref[k, rows : rows + 16, :] = tail.astype(BF)


def attend(q, ka, kb, va, vb, sa, sb, left):
    full = lambda n: pl.BlockSpec((n, HD), lambda i: (0, i))
    second = lambda n: pl.BlockSpec((n, HD), lambda i: (0, i + KV))
    return pl.pallas_call(
        attend_kernel,
        grid=(KV,),
        in_specs=[
            pl.BlockSpec((64, 4 * HD), lambda i: (0, i)),
            full(512),
            full(512),
            full(512),
            full(512),
            full(128),
            full(128),
            second(128),
            second(128),
            pl.BlockSpec((256, 2), lambda i: (0, 0)),
        ],
        out_specs=pl.BlockSpec((2, 80, 2 * HD), lambda i: (i, 0, 0)),
        out_shape=jax.ShapeDtypeStruct((16, 80, 2 * HD), BF),
        compiler_params=pltpu.CompilerParams(vmem_limit_bytes=16 * MB),
        cost_estimate=pl.CostEstimate(flops=1400000000, bytes_accessed=6 * MB, transcendentals=2700000),
    )(q, in_hbm(ka), in_hbm(kb), in_hbm(va), in_hbm(vb), sa, sb, sa, sb, left)


def columns_of(w_ref, half, buffer, sems):
    width = HALF // 4
    return [
        pltpu.make_async_copy(
            w_ref.at[:, pl.ds(pl.multiple_of(half * HALF + part * width, width), width)],
            buffer.at[:, pl.ds(part * width, width)],
            sems.at[part],
        )
        for part in range(4)
    ]


def project_parts(copies, attended, buffer, out_ref):
    width = HALF // 4
    for part, copy in enumerate(copies):
        copy.wait()
        at = slice(part * width, (part + 1) * width)
        out_ref[:, at] = dot(attended, buffer[:, at]).astype(BF)


def project_kernel(at_ref, got_ref, w_ref, out_ref, att_ref, buffer, sems):
    rows = 64
    copies = columns_of(w_ref, 1 - at_ref[0], buffer, sems)
    for copy in copies:
        copy.start()
    tops = [got_ref[s, rows : rows + 1, 0 : 2 * rows].astype(F32) for s in range(16)]
    sums = [
        got_ref[s, rows : rows + 1, 2 * rows :].astype(F32)
        + got_ref[s, rows + 1 : rows + 2, 2 * rows :].astype(F32)
        for s in range(16)
    ]
    top = functools.reduce(jnp.maximum, tops)
    factors = [jnp.exp2(t - top) for t in tops]
    total = functools.reduce(jnp.add, [f * s for f, s in zip(factors, sums)])
    lane = lax.broadcasted_iota(jnp.int32, (rows, 2 * rows), 1)
    line = lax.broadcasted_iota(jnp.int32, (rows, 2 * rows), 0)
    for j in range(2):
        here = lane == line + j * rows
        acc = jnp.zeros((rows, HD), F32)
        for s in range(16):
            share = jnp.sum(jnp.where(here, factors[s] / total, 0.0), axis=1, keepdims=True)
            acc = acc + got_ref[s, 0:rows, j * HD : (j + 1) * HD].astype(F32) * share
        att_ref[:, j * HD : (j + 1) * HD] = acc.astype(BF)
    project_parts(copies, att_ref[...], buffer, out_ref)


def project_other(at, got, w_out):
    return pl.pallas_call(
        project_kernel,
        in_specs=[
            pl.BlockSpec(memory_space=pltpu.SMEM),
            pl.BlockSpec(memory_space=pltpu.VMEM),
            pl.BlockSpec(memory_space=pl.ANY),
        ],
        out_specs=[pl.BlockSpec(memory_space=pltpu.VMEM)] * 2,
        out_shape=[jax.ShapeDtypeStruct((64, HALF), BF), jax.ShapeDtypeStruct((64, 256), BF)],
        scratch_shapes=[pltpu.VMEM((256, HALF), BF), pltpu.SemaphoreType.DMA((4,))],
        compiler_params=pltpu.CompilerParams(vmem_limit_bytes=16 * MB),
        cost_estimate=pl.CostEstimate(flops=140000000, bytes_accessed=3 * MB, transcendentals=0),
    )(at, got, in_hbm(w_out))


def project_mine_kernel(at_ref, att_ref, w_ref, out_ref, buffer, sems):
    copies = columns_of(w_ref, at_ref[0], buffer, sems)
    for copy in copies:
        copy.start()
    project_parts(copies, att_ref[...], buffer, out_ref)


def project_mine(at, attended, w_out):
    return pl.pallas_call(
        project_mine_kernel,
        in_specs=[
            pl.BlockSpec(memory_space=pltpu.SMEM),
            pl.BlockSpec(memory_space=pltpu.VMEM),
            pl.BlockSpec(memory_space=pl.ANY),
        ],
        out_specs=pl.BlockSpec(memory_space=pltpu.VMEM),
        out_shape=jax.ShapeDtypeStruct((64, HALF), BF),
        scratch_shapes=[pltpu.VMEM((256, HALF), BF), pltpu.SemaphoreType.DMA((4,))],
        compiler_params=pltpu.CompilerParams(vmem_limit_bytes=16 * MB),
        cost_estimate=pl.CostEstimate(flops=140000000, bytes_accessed=3 * MB, transcendentals=0),
    )(at, attended, in_hbm(w_out))


def rolled(place, back):
    return pl.multiple_of(((place + 4 - back) & 3) * 16, 16)


def first_kernel(at_ref, p0, p1, p2, p3, wg_ref, wu_ref, g_ref, u_ref):
    @pl.when(pl.program_id(0) == 0)
    def _():
        g_ref[...] = jnp.zeros_like(g_ref)
        u_ref[...] = jnp.zeros_like(u_ref)

    pieces = (p0, p1, p2, p3)
    x = jnp.concatenate(
        [pieces[a][pl.ds(rolled(at_ref[1], b), 16), :] for a in range(4) for b in range(4)], axis=0
    )
    g_ref[...] += dot(x, wg_ref[...])
    u_ref[...] += dot(x, wu_ref[...])


def expert_first(at, pieces, w_gate, w_up):
    units = w_gate.shape[1]
    block = 1024
    return pl.pallas_call(
        first_kernel,
        grid_spec=pltpu.PrefetchScalarGridSpec(
            num_scalar_prefetch=1,
            grid=(4,),
            in_specs=[pl.BlockSpec((64, block), lambda n, t: (0, n))] * 4
            + [pl.BlockSpec((block, units), lambda n, t: (n + 4 * t[0], 0))] * 2,
            out_specs=[pl.BlockSpec((256, units), lambda n, t: (0, 0))] * 2,
        ),
        out_shape=[jax.ShapeDtypeStruct((256, units), F32)] * 2,
        compiler_params=pltpu.CompilerParams(vmem_limit_bytes=12 * MB),
        cost_estimate=pl.CostEstimate(flops=16000000000, bytes_accessed=9 * MB, transcendentals=0),
    )(at, *pieces, in_vmem(w_gate), in_vmem(w_up))


def second_kernel(at_ref, p0, p1, p2, p3, wg_ref, wu_ref, g0_ref, u0_ref, wd_ref, inner_ref, out_ref, g_ref, u_ref):
    n = pl.program_id(0)

    @pl.when(n == 0)
    def _():
        g_ref[...] = g0_ref[...]
        u_ref[...] = u0_ref[...]

    @pl.when(n < 4)
    def _():
        pieces = (p0, p1, p2, p3)
        x = jnp.concatenate(
            [pieces[b][pl.ds(rolled(at_ref[2], a), 16), :] for a in range(4) for b in range(4)], axis=0
        )
        g_ref[...] += dot(x, wg_ref[...])
        u_ref[...] += dot(x, wu_ref[...])

    @pl.when(n == 3)
    def _():
        g = g_ref[...]
        inner_ref[...] = (g / (1.0 + jnp.exp(-g)) * u_ref[...]).astype(BF)

    @pl.when(n >= 4)
    def _():
        value = dot(inner_ref[...], wd_ref[...]).astype(BF)
        for a in range(4):
            for b in range(4):
                line = (4 * a + b) * 16
                out_ref[b, pl.ds(rolled(at_ref[2], a), 16), :] = value[line : line + 16]


def expert_second(at, pieces, w_gate, w_up, gate, up, w_down):
    units = w_gate.shape[1]
    block = 1024
    early = lambda n: jnp.minimum(n, 3)
    late = lambda n: jnp.maximum(n - 4, 0)
    whole = pl.BlockSpec((256, units), lambda n, t: (0, 0))
    return pl.pallas_call(
        second_kernel,
        grid_spec=pltpu.PrefetchScalarGridSpec(
            num_scalar_prefetch=1,
            grid=(8,),
            in_specs=[pl.BlockSpec((64, block), lambda n, t: (0, early(n)))] * 4
            + [pl.BlockSpec((block, units), lambda n, t: (early(n) + 4 * (1 - t[0]), 0))] * 2
            + [whole, whole, pl.BlockSpec((units, block), lambda n, t: (0, late(n) + 4 * (1 - t[0])))],
            out_specs=[whole, pl.BlockSpec((4, 64, block), lambda n, t: (0, 0, late(n)))],
            scratch_shapes=[pltpu.VMEM((256, units), F32), pltpu.VMEM((256, units), F32)],
        ),
        out_shape=[
            jax.ShapeDtypeStruct((256, units), BF),
            jax.ShapeDtypeStruct((4, 64, HALF), BF),
        ],
        compiler_params=pltpu.CompilerParams(vmem_limit_bytes=12 * MB),
        cost_estimate=pl.CostEstimate(flops=2400000000, bytes_accessed=15 * MB, transcendentals=0),
    )(at, *pieces, in_vmem(w_gate), in_vmem(w_up), gate, up, in_vmem(w_down))


def third_kernel(at_ref, inner_ref, wd_ref, out_ref):
    value = dot(inner_ref[...], wd_ref[...]).astype(BF)
    for a in range(4):
        for b in range(4):
            line = (4 * a + b) * 16
            out_ref[a, pl.ds(rolled(at_ref[1], b), 16), :] = value[line : line + 16]


def expert_third(at, inner, w_down):
    rows, units = inner.shape
    block = 1024
    return pl.pallas_call(
        third_kernel,
        grid_spec=pltpu.PrefetchScalarGridSpec(
            num_scalar_prefetch=1,
            grid=(4,),
            in_specs=[
                pl.BlockSpec((rows, units), lambda n, t: (0, 0)),
                pl.BlockSpec((units, block), lambda n, t: (0, n + 4 * t[0])),
            ],
            out_specs=pl.BlockSpec((4, 64, block), lambda n, t: (0, 0, n)),
        ),
        out_shape=jax.ShapeDtypeStruct((4, 64, HALF), BF),
        compiler_params=pltpu.CompilerParams(vmem_limit_bytes=12 * MB),
        cost_estimate=pl.CostEstimate(flops=800000000, bytes_accessed=6 * MB, transcendentals=0),
    )(at, inner, in_vmem(w_down))


def swap(value):
    return lax.ppermute(value, "c", SWAP)


def local(
    queries,
    prefix_keys,
    prefix_values,
    suffix_keys,
    suffix_values,
    suffix_lengths,
    hidden_in,
    w_out,
    norm_gain,
    expert_ids,
    expert_weights,
    w_gate,
    w_up,
    w_down,
):
    c = lax.axis_index("c").astype(jnp.int32)
    z = lax.axis_index("z").astype(jnp.int32)
    y = lax.axis_index("y").astype(jnp.int32)
    chip = 4 * z + y
    at = jnp.stack([c, jnp.where(c == 0, z, y), jnp.where(c == 0, y, z)])

    def in_order(own, got, axis):
        return jnp.where(
            c == 0, jnp.concatenate([own, got], axis=axis), jnp.concatenate([got, own], axis=axis)
        )

    q = queries.reshape(2, 16, 2, 2 * HD).transpose(2, 0, 1, 3).reshape(1, 2, 2, HALF)
    q = jnp.broadcast_to(q, (16, 2, 2, HALF)).reshape(32, 2, HALF)
    keys_b = swap(prefix_keys)
    values_b = swap(prefix_values)
    suffix_keys_b = swap(suffix_keys)
    suffix_values_b = swap(suffix_values)
    q = lax.all_to_all(q, PLANE, split_axis=0, concat_axis=0, tiled=True).reshape(64, HALF)
    suffix = jnp.concatenate([suffix_keys, suffix_values], axis=-1).reshape(128, 2 * KV * HD)
    suffix_b = jnp.concatenate([suffix_keys_b, suffix_values_b], axis=-1).reshape(128, 2 * KV * HD)
    first = 4 * chip
    left = jnp.stack([suffix_lengths - (first + 2 * c), suffix_lengths - (first + 2 * (1 - c))], axis=1)
    left = jnp.tile(left.astype(jnp.int32), (4, 1))
    hidden = in_order(
        lax.dynamic_slice_in_dim(hidden_in, c * HALF, HALF, 1),
        swap(lax.dynamic_slice_in_dim(hidden_in, (1 - c) * HALF, HALF, 1)),
        0,
    ).astype(F32)
    match = expert_ids[:, :, None] == jnp.arange(4, dtype=jnp.int32)[None, None, :]
    weights = jnp.sum(jnp.where(match, expert_weights[:, :, None], 0.0), axis=1)
    weights = in_order(weights, swap(weights), 0)
    gain = lax.dynamic_slice_in_dim(norm_gain, c * HALF, HALF, 0).astype(F32)

    parts = attend(q, prefix_keys, keys_b, prefix_values, values_b, suffix, suffix_b, left)
    parts = lax.all_to_all(parts, ("z", "y"), split_axis=0, concat_axis=0, tiled=True)
    other, attended = project_other(at, parts, w_out)
    other = swap(other)
    mine = project_mine(at, attended, w_out)
    summed = (mine.astype(F32) + other.astype(F32)).astype(BF).reshape(16, 4, HALF)
    summed = lax.all_to_all(summed, ("z", "y"), split_axis=0, concat_axis=0, tiled=True)
    residual = hidden + jnp.sum(summed.astype(F32), axis=0)
    square = jnp.sum(residual * residual, axis=-1, keepdims=True)
    mean_square = (square + swap(square)) * (1.0 / D)
    normed = (residual * lax.rsqrt(mean_square + EPS) * gain).astype(BF)
    wide = wide_groups()
    sent = jnp.broadcast_to(normed[None], (16, 4, HALF))
    own = lax.all_to_all(
        sent, ALL, split_axis=0, concat_axis=0, tiled=True, axis_index_groups=wide
    ).reshape(64, HALF)
    pieces = [own] + [lax.ppermute(own, PLANE, line_shift(s)) for s in (1, 2, 3)]
    w_gate, w_up, w_down = fetch(own, w_gate[0], w_up[0], w_down[0])
    pieces_b = [swap(piece) for piece in pieces]
    gate, up = expert_first(at, pieces, w_gate, w_up)
    inner, other_out = expert_second(at, pieces_b, w_gate, w_up, gate, up, w_down)
    other_out = swap(other_out)
    mine_out = expert_third(at, inner, w_down)
    out = [(mine_out[s].astype(F32) + other_out[s].astype(F32)).astype(BF) for s in range(4)]
    out = [out[0]] + [lax.ppermute(out[s], PLANE, line_shift(4 - s)) for s in (1, 2, 3)]
    out = functools.reduce(jnp.add, [piece.astype(F32) for piece in out]).astype(BF)
    out = lax.all_to_all(
        out.reshape(16, 4, HALF), ALL, split_axis=0, concat_axis=0, tiled=True, axis_index_groups=wide
    )
    out = out.reshape(4, 4, 4, HALF).astype(F32)
    mixed = residual + jnp.sum(out * weights.T[None, :, :, None], axis=(0, 1))
    mixed = mixed.astype(BF)
    kept = lax.dynamic_slice_in_dim(mixed, 2 * c, 2, 0)
    got = swap(lax.dynamic_slice_in_dim(mixed, 2 * (1 - c), 2, 0))
    return in_order(kept, got, 1)


def solution(mesh):
    grid = Mesh(mesh.devices.reshape(4, 4, 4, 2), ALL)
    placed = (
        P(ALL, None),
        P(PLANE, None),
        P(PLANE, None),
        P("x", PLANE, None),
        P("x", PLANE, None),
        P("x"),
        P(ALL, None),
        P(PLANE, None),
        P(),
        P(ALL, None),
        P(ALL, None),
        P("x", None, PLANE),
        P("x", None, PLANE),
        P("x", PLANE, None),
    )
    return jax.shard_map(
        local, mesh=grid, in_specs=placed, out_specs=P(ALL, None), check_vma=False
    )
```

```python
import functools

import jax
import jax.numpy as jnp
from jax import lax
from jax.experimental import pallas as pl
from jax.experimental.pallas import tpu as pltpu
from jax.sharding import Mesh, PartitionSpec as P

HEADS = 64
KV = 8
HD = 128
D = 8192
HALF = D // 2
EPS = 1e-05
NEG = -1e30
LOG2E = 1.4426950408889634
SCALE = LOG2E / HD**0.5
BF = jnp.bfloat16
F32 = jnp.float32
ALL = ("x", "z", "y", "c")
PLANE = ("z", "y", "c")
SWAP = [(0, 1), (1, 0)]
MB = 1 << 20
WHOLE = pl.BlockSpec(memory_space=pltpu.VMEM)
SCALARS = pl.BlockSpec(memory_space=pltpu.SMEM)


def device(x, z, y, c):
    return ((x * 4 + z) * 4 + y) * 2 + c


def wide_groups():
    four = range(4)
    zeros = [[device(x, z, y, 0) for z in four for x in four] for y in four]
    return zeros + [[device(x, z, y, 1) for y in four for x in four] for z in four]


def line_shift(step):
    pairs = []
    for z in range(4):
        for y in range(4):
            pairs.append(((z * 4 + y) * 2, (z * 4 + (y + step) % 4) * 2))
            pairs.append(((z * 4 + y) * 2 + 1, (((z + step) % 4) * 4 + y) * 2 + 1))
    return pairs


def dot(a, b):
    return jnp.dot(a, b, preferred_element_type=F32)


def dot_t(a, b):
    return lax.dot_general(a, b, (((1,), (1,)), ((), ())), preferred_element_type=F32)


def fetch_kernel(at_ref, after_ref, wg_ref, wu_ref, wd_ref, wdb_ref, gate_up_ref, down_ref, sems):
    units = wg_ref.shape[1]
    pairs = []
    for part in range(4):
        rows = pl.ds(part * D // 4, D // 4)
        pairs.append((wg_ref.at[rows], gate_up_ref.at[rows, pl.ds(0, units)]))
        pairs.append((wu_ref.at[rows], gate_up_ref.at[rows, pl.ds(units, units)]))
    columns = pl.ds(pl.multiple_of(at_ref[0] * HALF, HALF), HALF)
    for part in range(2):
        rows = pl.ds(part * units // 2, units // 2)
        pairs.append((wd_ref.at[rows, columns], down_ref.at[rows]))
        rows_b = pl.ds(units + part * units // 2, units // 2)
        pairs.append((wdb_ref.at[rows, columns], down_ref.at[rows_b]))
    copies = [pltpu.make_async_copy(src, dst, sems.at[i]) for i, (src, dst) in enumerate(pairs)]
    for copy in copies:
        copy.start()
    for copy in copies:
        copy.wait()


def fetch(at, after, w_gate, w_up, w_down, w_down_b):
    units = w_gate.shape[1]
    return pl.pallas_call(
        fetch_kernel,
        in_specs=[SCALARS] + [pl.BlockSpec(memory_space=pl.ANY)] * 5,
        out_specs=[WHOLE] * 2,
        out_shape=[pltpu.VMEM((D, 2 * units), BF), pltpu.VMEM((2 * units, HALF), BF)],
        scratch_shapes=[pltpu.SemaphoreType.DMA((12,))],
        compiler_params=pltpu.CompilerParams(vmem_limit_bytes=4 * MB),
        cost_estimate=pl.CostEstimate(flops=0, bytes_accessed=22 * MB, transcendentals=0),
    )(at, after, in_hbm(w_gate), in_hbm(w_up), in_hbm(w_down), in_hbm(w_down_b))


def in_vmem(array):
    return pltpu.with_memory_space_constraint(array, pltpu.VMEM)


def in_hbm(array):
    return pltpu.with_memory_space_constraint(array, pltpu.HBM)


def spread_kernel(q_ref, out_ref):
    for half in range(2):
        value = jnp.concatenate(
            [q_ref[:, (2 * k + half) * 2 * HD : (2 * k + half + 1) * 2 * HD] for k in range(16)], axis=1
        )
        for chip in range(16):
            out_ref[2 * chip + half] = value


def spread(queries):
    return pl.pallas_call(
        spread_kernel,
        in_specs=[WHOLE],
        out_specs=WHOLE,
        out_shape=jax.ShapeDtypeStruct((32, 2, HALF), BF),
        compiler_params=pltpu.CompilerParams(vmem_limit_bytes=4 * MB),
        cost_estimate=pl.CostEstimate(flops=0, bytes_accessed=MB, transcendentals=0),
    )(queries)


def attend_kernel(q_ref, ka_ref, kb_ref, va_ref, vb_ref, sa_ref, sb_ref, left_ref, out_ref):
    rows = 64
    row = lax.broadcasted_iota(jnp.int32, (4 * rows, 4 * rows), 0)
    col = lax.broadcasted_iota(jnp.int32, (4 * rows, 4 * rows), 1)
    left = left_ref[...]
    live = (row % rows == col % (2 * rows) // 2) & (
        col % 2 < jnp.where(col < 2 * rows, left[:, 0:1], left[:, 1:2])
    )
    eye = row == col
    line = lax.broadcasted_iota(jnp.int32, (16, 4 * rows), 0)
    for h in range(KV):
        at = slice(h * HD, (h + 1) * HD)
        at_v = slice((KV + h) * HD, (KV + h + 1) * HD)
        q = jnp.concatenate(
            [q_ref[:, (4 * h + g) * HD : (4 * h + g + 1) * HD] for g in range(4)], axis=0
        )
        suffix_k = jnp.concatenate([sa_ref[:, at], sb_ref[:, at]], axis=0)
        suffix_v = jnp.concatenate([sa_ref[:, at_v], sb_ref[:, at_v]], axis=0)
        scores = [
            dot_t(q, ka_ref[:, at]),
            dot_t(q, kb_ref[:, at]),
            jnp.where(live, dot_t(q, suffix_k), NEG),
        ]
        top = functools.reduce(jnp.maximum, [jnp.max(s, axis=1, keepdims=True) for s in scores])
        top = (top * SCALE).astype(BF).astype(F32)
        total = jnp.zeros((4 * rows, 1), F32)
        acc = jnp.zeros((4 * rows, HD), F32)
        for s, v in zip(scores, (va_ref[:, at], vb_ref[:, at], suffix_v)):
            prob = jnp.exp2(s * SCALE - top)
            total = total + jnp.sum(prob, axis=1, keepdims=True)
            acc = acc + dot(prob.astype(BF), v)
        top_row = jnp.sum(jnp.where(eye, top, 0.0), axis=0, keepdims=True)
        total_row = jnp.sum(jnp.where(eye, total, 0.0), axis=0, keepdims=True)
        total_high = total_row.astype(BF).astype(F32)
        total_low = total_row - total_high
        for k in range(2):
            for j in range(2):
                g = 2 * k + j
                out_ref[2 * h + k, 0:rows, j * HD : (j + 1) * HD] = acc[
                    g * rows : (g + 1) * rows
                ].astype(BF)
            part = slice(k * 2 * rows, (k + 1) * 2 * rows)
            high = jnp.concatenate([top_row[:, part], total_high[:, part]], axis=1)
            low = jnp.concatenate([top_row[:, part], total_low[:, part]], axis=1)
            tail = jnp.where(line == 0, high, jnp.where(line == 1, low, 0.0))
            out_ref[2 * h + k, rows : rows + 16, :] = tail.astype(BF)


def attend(q, ka, kb, va, vb, sa, sb, left):
    arrays = (q, ka, kb, va, vb, sa, sb, left)
    return pl.pallas_call(
        attend_kernel,
        grid=(1,),
        in_specs=[pl.BlockSpec(a.shape, lambda i: (0, 0)) for a in arrays],
        out_specs=pl.BlockSpec((16, 80, 2 * HD), lambda i: (0, 0, 0)),
        out_shape=jax.ShapeDtypeStruct((16, 80, 2 * HD), BF),
        compiler_params=pltpu.CompilerParams(vmem_limit_bytes=24 * MB),
        cost_estimate=pl.CostEstimate(flops=1400000000, bytes_accessed=6 * MB, transcendentals=2700000),
    )(q, in_hbm(ka), kb, in_hbm(va), vb, sa, sb, left)


def columns_of(w_ref, half, buffer, sems):
    width = HALF // 4
    return [
        pltpu.make_async_copy(
            w_ref.at[:, pl.ds(pl.multiple_of(half * HALF + part * width, width), width)],
            buffer.at[:, pl.ds(part * width, width)],
            sems.at[part],
        )
        for part in range(4)
    ]


def project_parts(copies, attended, buffer, out_ref):
    width = HALF // 4
    for part, copy in enumerate(copies):
        copy.wait()
        at = slice(part * width, (part + 1) * width)
        out_ref[:, at] = dot(attended, buffer[:, at]).astype(BF)


def project_kernel(at_ref, got_ref, w_ref, early_ref, out_ref, att_ref, buffer, sems):
    rows = 64
    copies = columns_of(w_ref, 1 - at_ref[0], buffer, sems)
    for copy in copies:
        copy.start()
    tops = [got_ref[s, rows : rows + 1, 0 : 2 * rows].astype(F32) for s in range(16)]
    sums = [
        got_ref[s, rows : rows + 1, 2 * rows :].astype(F32)
        + got_ref[s, rows + 1 : rows + 2, 2 * rows :].astype(F32)
        for s in range(16)
    ]
    top = functools.reduce(jnp.maximum, tops)
    factors = [jnp.exp2(t - top) for t in tops]
    total = functools.reduce(jnp.add, [f * s for f, s in zip(factors, sums)])
    lane = lax.broadcasted_iota(jnp.int32, (rows, 2 * rows), 1)
    line = lax.broadcasted_iota(jnp.int32, (rows, 2 * rows), 0)
    for j in range(2):
        here = lane == line + j * rows
        acc = jnp.zeros((rows, HD), F32)
        for s in range(16):
            share = jnp.sum(jnp.where(here, factors[s] / total, 0.0), axis=1, keepdims=True)
            acc = acc + got_ref[s, 0:rows, j * HD : (j + 1) * HD].astype(F32) * share
        att_ref[:, j * HD : (j + 1) * HD] = acc.astype(BF)
    project_parts(copies, att_ref[...], buffer, out_ref)


def project_other(at, got, w_out, early):
    return pl.pallas_call(
        project_kernel,
        in_specs=[
            pl.BlockSpec(memory_space=pltpu.SMEM),
            pl.BlockSpec(memory_space=pltpu.VMEM),
            pl.BlockSpec(memory_space=pl.ANY),
            pl.BlockSpec(memory_space=pl.ANY),
        ],
        out_specs=[pl.BlockSpec(memory_space=pltpu.VMEM)] * 2,
        out_shape=[jax.ShapeDtypeStruct((64, HALF), BF), jax.ShapeDtypeStruct((64, 256), BF)],
        scratch_shapes=[pltpu.VMEM((256, HALF), BF), pltpu.SemaphoreType.DMA((4,))],
        compiler_params=pltpu.CompilerParams(vmem_limit_bytes=16 * MB),
        cost_estimate=pl.CostEstimate(flops=140000000, bytes_accessed=3 * MB, transcendentals=0),
    )(at, got, in_hbm(w_out), in_hbm(early))


def project_mine_kernel(at_ref, att_ref, w_ref, out_ref, buffer, sems):
    copies = columns_of(w_ref, at_ref[0], buffer, sems)
    for copy in copies:
        copy.start()
    project_parts(copies, att_ref[...], buffer, out_ref)


def project_mine(at, attended, w_out):
    return pl.pallas_call(
        project_mine_kernel,
        in_specs=[
            pl.BlockSpec(memory_space=pltpu.SMEM),
            pl.BlockSpec(memory_space=pltpu.VMEM),
            pl.BlockSpec(memory_space=pl.ANY),
        ],
        out_specs=pl.BlockSpec(memory_space=pltpu.VMEM),
        out_shape=jax.ShapeDtypeStruct((64, HALF), BF),
        scratch_shapes=[pltpu.VMEM((256, HALF), BF), pltpu.SemaphoreType.DMA((4,))],
        compiler_params=pltpu.CompilerParams(vmem_limit_bytes=16 * MB),
        cost_estimate=pl.CostEstimate(flops=140000000, bytes_accessed=3 * MB, transcendentals=0),
    )(at, attended, in_hbm(w_out))


def rolled(place, back):
    return pl.multiple_of(((place + 4 - back) & 3) * 16, 16)


def gathered(x_ref, pieces, place, own):
    for a in range(4):
        for b in range(4):
            piece, back = (a, b) if own else (b, a)
            line = (4 * a + b) * 16
            x_ref[line : line + 16, :] = pieces[piece][pl.ds(rolled(place, back), 16), :]


def multiplied(x_ref, w_ref, half, acc_ref):
    width = HALF // 4
    for part in range(4):
        rows = pl.ds(pl.multiple_of(half * HALF + part * width, width), width)
        value = dot(x_ref[:, part * width : (part + 1) * width], w_ref[rows, :])
        if part == 0:
            acc_ref[...] = value
        else:
            acc_ref[...] += value


def first_kernel(at_ref, p0, p1, p2, p3, w_ref, acc_ref, x_ref):
    gathered(x_ref, (p0, p1, p2, p3), at_ref[1], True)
    multiplied(x_ref, w_ref, at_ref[0], acc_ref)


def expert_first(at, pieces, gate_up):
    units = gate_up.shape[1]
    return pl.pallas_call(
        first_kernel,
        in_specs=[SCALARS] + [WHOLE] * 5,
        out_specs=WHOLE,
        out_shape=jax.ShapeDtypeStruct((256, units), F32),
        scratch_shapes=[pltpu.VMEM((256, HALF), BF)],
        compiler_params=pltpu.CompilerParams(vmem_limit_bytes=12 * MB),
        cost_estimate=pl.CostEstimate(flops=16000000000, bytes_accessed=9 * MB, transcendentals=0),
    )(at, *pieces, in_vmem(gate_up))


def second_kernel(at_ref, p0, p1, p2, p3, w_ref, acc_ref, inner_ref, x_ref, more_ref):
    units = inner_ref.shape[1]
    gathered(x_ref, (p0, p1, p2, p3), at_ref[2], False)
    multiplied(x_ref, w_ref, 1 - at_ref[0], more_ref)
    gate = acc_ref[:, :units] + more_ref[:, :units]
    up = acc_ref[:, units:] + more_ref[:, units:]
    inner_ref[...] = (gate / (1.0 + jnp.exp(-gate)) * up).astype(BF)


def expert_second(at, pieces, gate_up, acc):
    units = gate_up.shape[1]
    return pl.pallas_call(
        second_kernel,
        in_specs=[SCALARS] + [WHOLE] * 6,
        out_specs=WHOLE,
        out_shape=jax.ShapeDtypeStruct((256, units // 2), BF),
        scratch_shapes=[pltpu.VMEM((256, HALF), BF), pltpu.VMEM((256, units), F32)],
        compiler_params=pltpu.CompilerParams(vmem_limit_bytes=12 * MB),
        cost_estimate=pl.CostEstimate(flops=1600000000, bytes_accessed=9 * MB, transcendentals=0),
    )(at, *pieces, in_vmem(gate_up), acc)


def third_kernel(at_ref, inner_ref, other_ref, w_ref, o0, o1, o2, o3, x_ref):
    units = inner_ref.shape[1]
    x_ref[:, :units] = inner_ref[...]
    for a in range(4):
        for b in range(4):
            line, line_b = (4 * a + b) * 16, (4 * b + a) * 16
            x_ref[line : line + 16, units:] = other_ref[line_b : line_b + 16, :]
    outs = (o0, o1, o2, o3)
    width = HALF // 4
    for part in range(4):
        cols = slice(part * width, (part + 1) * width)
        value = dot(x_ref[...], w_ref[:, cols]).astype(BF)
        for a in range(4):
            for b in range(4):
                line = (4 * a + b) * 16
                outs[a][pl.ds(rolled(at_ref[1], b), 16), cols] = value[line : line + 16]


def expert_third(at, inner, other, down):
    units = inner.shape[1]
    return pl.pallas_call(
        third_kernel,
        in_specs=[SCALARS] + [WHOLE] * 3,
        out_specs=[WHOLE] * 4,
        out_shape=[jax.ShapeDtypeStruct((64, HALF), BF)] * 4,
        scratch_shapes=[pltpu.VMEM((256, 2 * units), BF)],
        compiler_params=pltpu.CompilerParams(vmem_limit_bytes=12 * MB),
        cost_estimate=pl.CostEstimate(flops=1600000000, bytes_accessed=9 * MB, transcendentals=0),
    )(at, inner, other, in_vmem(down))


def swap(value):
    return lax.ppermute(value, "c", SWAP)


def local(
    queries,
    prefix_keys,
    prefix_values,
    suffix_keys,
    suffix_values,
    suffix_lengths,
    hidden_in,
    w_out,
    norm_gain,
    expert_ids,
    expert_weights,
    w_gate,
    w_up,
    w_down,
):
    c = lax.axis_index("c").astype(jnp.int32)
    z = lax.axis_index("z").astype(jnp.int32)
    y = lax.axis_index("y").astype(jnp.int32)
    chip = 4 * z + y
    at = jnp.stack([c, jnp.where(c == 0, z, y), jnp.where(c == 0, y, z)])

    def in_order(own, got, axis):
        return jnp.where(
            c == 0, jnp.concatenate([own, got], axis=axis), jnp.concatenate([got, own], axis=axis)
        )

    q = spread(queries)
    keys_b = swap(prefix_keys)
    values_b = swap(prefix_values)
    suffix_keys_b = swap(suffix_keys)
    suffix_values_b = swap(suffix_values)
    w_down_b = swap(w_down[0])
    q = lax.all_to_all(q, PLANE, split_axis=0, concat_axis=0, tiled=True).reshape(64, HALF)
    suffix = jnp.concatenate([suffix_keys, suffix_values], axis=-1).reshape(128, 2 * KV * HD)
    suffix_b = jnp.concatenate([suffix_keys_b, suffix_values_b], axis=-1).reshape(128, 2 * KV * HD)
    first = 4 * chip
    left = jnp.stack([suffix_lengths - (first + 2 * c), suffix_lengths - (first + 2 * (1 - c))], axis=1)
    left = jnp.tile(left.astype(jnp.int32), (4, 1))
    hidden = in_order(
        lax.dynamic_slice_in_dim(hidden_in, c * HALF, HALF, 1),
        swap(lax.dynamic_slice_in_dim(hidden_in, (1 - c) * HALF, HALF, 1)),
        0,
    ).astype(F32)
    match = expert_ids[:, :, None] == jnp.arange(4, dtype=jnp.int32)[None, None, :]
    weights = jnp.sum(jnp.where(match, expert_weights[:, :, None], 0.0), axis=1)
    weights = in_order(weights, swap(weights), 0)
    gain = lax.dynamic_slice_in_dim(norm_gain, c * HALF, HALF, 0).astype(F32)

    parts = attend(q, prefix_keys, keys_b, prefix_values, values_b, suffix, suffix_b, left)
    parts = lax.all_to_all(parts, ("z", "y"), split_axis=0, concat_axis=0, tiled=True)
    other, attended = project_other(at, parts, w_out, w_down_b)
    other = swap(other)
    mine = project_mine(at, attended, w_out)
    summed = (mine.astype(F32) + other.astype(F32)).astype(BF).reshape(16, 4, HALF)
    summed = lax.all_to_all(summed, ("z", "y"), split_axis=0, concat_axis=0, tiled=True)
    residual = hidden + jnp.sum(summed.astype(F32), axis=0)
    square = jnp.sum(residual * residual, axis=-1, keepdims=True)
    mean_square = (square + swap(square)) * (1.0 / D)
    normed = (residual * lax.rsqrt(mean_square + EPS) * gain).astype(BF)
    wide = wide_groups()
    sent = jnp.broadcast_to(normed[None], (16, 4, HALF))
    own = lax.all_to_all(
        sent, ALL, split_axis=0, concat_axis=0, tiled=True, axis_index_groups=wide
    ).reshape(64, HALF)
    pieces = [own] + [lax.ppermute(own, PLANE, line_shift(s)) for s in (1, 2, 3)]
    gate_up, down = fetch(at, own, w_gate[0], w_up[0], w_down[0], w_down_b)
    pieces_b = [swap(piece) for piece in pieces]
    acc = expert_first(at, pieces, gate_up)
    inner = expert_second(at, pieces_b, gate_up, acc)
    out = expert_third(at, inner, swap(inner), down)
    out = [out[0]] + [lax.ppermute(out[s], PLANE, line_shift(4 - s)) for s in (1, 2, 3)]
    out = functools.reduce(jnp.add, [piece.astype(F32) for piece in out]).astype(BF)
    out = lax.all_to_all(
        out.reshape(16, 4, HALF), ALL, split_axis=0, concat_axis=0, tiled=True, axis_index_groups=wide
    )
    out = out.reshape(4, 4, 4, HALF).astype(F32)
    mixed = residual + jnp.sum(out * weights.T[None, :, :, None], axis=(0, 1))
    mixed = mixed.astype(BF)
    kept = lax.dynamic_slice_in_dim(mixed, 2 * c, 2, 0)
    got = swap(lax.dynamic_slice_in_dim(mixed, 2 * (1 - c), 2, 0))
    return in_order(kept, got, 1)


def solution(mesh):
    grid = Mesh(mesh.devices.reshape(4, 4, 4, 2), ALL)
    placed = (
        P(ALL, None),
        P(PLANE, None),
        P(PLANE, None),
        P("x", PLANE, None),
        P("x", PLANE, None),
        P("x"),
        P(ALL, None),
        P(PLANE, None),
        P(),
        P(ALL, None),
        P(ALL, None),
        P("x", None, PLANE),
        P("x", None, PLANE),
        P("x", PLANE, None),
    )
    return jax.shard_map(
        local, mesh=grid, in_specs=placed, out_specs=P(ALL, None), check_vma=False
    )
```

```python
import functools

import jax
import jax.numpy as jnp
from jax import lax
from jax.experimental import pallas as pl
from jax.experimental.pallas import tpu as pltpu
from jax.sharding import Mesh, PartitionSpec as P

HEADS = 64
KV = 8
HD = 128
D = 8192
HALF = D // 2
EPS = 1e-05
NEG = -1e30
LOG2E = 1.4426950408889634
SCALE = LOG2E / HD**0.5
BF = jnp.bfloat16
F32 = jnp.float32
ALL = ("x", "z", "y", "c")
PLANE = ("z", "y", "c")
SWAP = [(0, 1), (1, 0)]
MB = 1 << 20
WHOLE = pl.BlockSpec(memory_space=pltpu.VMEM)
SCALARS = pl.BlockSpec(memory_space=pltpu.SMEM)


def device(x, z, y, c):
    return ((x * 4 + z) * 4 + y) * 2 + c


def wide_groups():
    four = range(4)
    zeros = [[device(x, z, y, 0) for z in four for x in four] for y in four]
    return zeros + [[device(x, z, y, 1) for y in four for x in four] for z in four]


def line_shift(step):
    pairs = []
    for z in range(4):
        for y in range(4):
            pairs.append(((z * 4 + y) * 2, (z * 4 + (y + step) % 4) * 2))
            pairs.append(((z * 4 + y) * 2 + 1, (((z + step) % 4) * 4 + y) * 2 + 1))
    return pairs


def dot(a, b):
    return jnp.dot(a, b, preferred_element_type=F32)


def dot_t(a, b):
    return lax.dot_general(a, b, (((1,), (1,)), ((), ())), preferred_element_type=F32)


def fetch_kernel(at_ref, after_ref, wg_ref, wu_ref, wd_ref, wdb_ref, gate_up_ref, down_ref, sems):
    units = wg_ref.shape[1]
    pairs = []
    for part in range(4):
        rows = pl.ds(part * D // 4, D // 4)
        pairs.append((wg_ref.at[rows], gate_up_ref.at[rows, pl.ds(0, units)]))
        pairs.append((wu_ref.at[rows], gate_up_ref.at[rows, pl.ds(units, units)]))
    columns = pl.ds(pl.multiple_of(at_ref[0] * HALF, HALF), HALF)
    for part in range(2):
        rows = pl.ds(part * units // 2, units // 2)
        pairs.append((wd_ref.at[rows, columns], down_ref.at[rows]))
        rows_b = pl.ds(units + part * units // 2, units // 2)
        pairs.append((wdb_ref.at[rows, columns], down_ref.at[rows_b]))
    copies = [pltpu.make_async_copy(src, dst, sems.at[i]) for i, (src, dst) in enumerate(pairs)]
    for copy in copies:
        copy.start()
    for copy in copies:
        copy.wait()


def fetch(at, after, w_gate, w_up, w_down, w_down_b):
    units = w_gate.shape[1]
    return pl.pallas_call(
        fetch_kernel,
        in_specs=[SCALARS] + [pl.BlockSpec(memory_space=pl.ANY)] * 5,
        out_specs=[WHOLE] * 2,
        out_shape=[pltpu.VMEM((D, 2 * units), BF), pltpu.VMEM((2 * units, HALF), BF)],
        scratch_shapes=[pltpu.SemaphoreType.DMA((12,))],
        compiler_params=pltpu.CompilerParams(vmem_limit_bytes=4 * MB),
        cost_estimate=pl.CostEstimate(flops=0, bytes_accessed=22 * MB, transcendentals=0),
    )(at, after, in_hbm(w_gate), in_hbm(w_up), in_hbm(w_down), in_hbm(w_down_b))


def in_vmem(array):
    return pltpu.with_memory_space_constraint(array, pltpu.VMEM)


def in_hbm(array):
    return pltpu.with_memory_space_constraint(array, pltpu.HBM)


def spread_kernel(q_ref, hidden_ref, out_ref, copy_ref):
    copy_ref[...] = hidden_ref[...]
    for half in range(2):
        value = jnp.concatenate(
            [q_ref[:, (2 * k + half) * 2 * HD : (2 * k + half + 1) * 2 * HD] for k in range(16)], axis=1
        )
        for chip in range(16):
            out_ref[2 * chip + half] = value


def spread(queries, hidden):
    whole = pl.BlockSpec((2, D), lambda i: (0, 0))
    return pl.pallas_call(
        spread_kernel,
        grid=(1,),
        in_specs=[whole] * 2,
        out_specs=[pl.BlockSpec((32, 2, HALF), lambda i: (0, 0, 0)), whole],
        out_shape=[jax.ShapeDtypeStruct((32, 2, HALF), BF), jax.ShapeDtypeStruct((2, D), BF)],
        compiler_params=pltpu.CompilerParams(vmem_limit_bytes=4 * MB),
        cost_estimate=pl.CostEstimate(flops=0, bytes_accessed=MB, transcendentals=0),
    )(in_hbm(queries), in_hbm(hidden))


def store_part(out_ref, first, acc, top, total):
    rows = 64
    size = (4 * rows, 4 * rows)
    eye = lax.broadcasted_iota(jnp.int32, size, 0) == lax.broadcasted_iota(jnp.int32, size, 1)
    top_row = jnp.sum(jnp.where(eye, top, 0.0), axis=0, keepdims=True)
    total_row = jnp.sum(jnp.where(eye, total, 0.0), axis=0, keepdims=True)
    total_high = total_row.astype(BF).astype(F32)
    total_low = total_row - total_high
    line = lax.broadcasted_iota(jnp.int32, (8, 4 * rows), 0)
    for k in range(2):
        for j in range(2):
            g = 2 * k + j
            out_ref[first + k, 0:rows, j * HD : (j + 1) * HD] = acc[g * rows : (g + 1) * rows].astype(BF)
        part = slice(k * 2 * rows, (k + 1) * 2 * rows)
        high = jnp.concatenate([top_row[:, part], total_high[:, part]], axis=1)
        low = jnp.concatenate([top_row[:, part], total_low[:, part]], axis=1)
        tail = jnp.where(line == 0, high, jnp.where(line == 1, low, 0.0))
        out_ref[first + k, rows : rows + 8, :] = tail.astype(BF)


def attend_kernel(q_ref, ka_ref, kb_ref, va_ref, vb_ref, sa_ref, sb_ref, left_ref, *refs):
    out_ref = refs[-1]
    rows = 64
    row = lax.broadcasted_iota(jnp.int32, (4 * rows, 4 * rows), 0)
    col = lax.broadcasted_iota(jnp.int32, (4 * rows, 4 * rows), 1)
    left = left_ref[...]
    live = (row % rows == col % (2 * rows) // 2) & (
        col % 2 < jnp.where(col < 2 * rows, left[:, 0:1], left[:, 1:2])
    )
    for h in range(KV):
        at = slice(h * HD, (h + 1) * HD)
        at_v = slice((KV + h) * HD, (KV + h + 1) * HD)
        q = jnp.concatenate(
            [q_ref[:, (4 * h + g) * HD : (4 * h + g + 1) * HD] for g in range(4)], axis=0
        )
        suffix_k = jnp.concatenate([sa_ref[:, at], sb_ref[:, at]], axis=0)
        suffix_v = jnp.concatenate([sa_ref[:, at_v], sb_ref[:, at_v]], axis=0)
        scores = [
            dot_t(q, ka_ref[:, at]),
            dot_t(q, kb_ref[:, at]),
            jnp.where(live, dot_t(q, suffix_k), NEG),
        ]
        top = functools.reduce(jnp.maximum, [jnp.max(s, axis=1, keepdims=True) for s in scores])
        top = (top * SCALE).astype(BF).astype(F32)
        total, acc = 0.0, 0.0
        for s, v in zip(scores, (va_ref[:, at], vb_ref[:, at], suffix_v)):
            prob = jnp.exp2(s * SCALE - top)
            total = total + jnp.sum(prob, axis=1, keepdims=True)
            acc = acc + dot(prob.astype(BF), v)
        store_part(out_ref, 2 * h, acc, top, total)


def attend(q, ka, kb, va, vb, sa, sb, left, early):
    arrays = (q, ka, kb, va, vb, sa, sb, left)
    return pl.pallas_call(
        attend_kernel,
        grid=(1,),
        in_specs=[pl.BlockSpec(a.shape, lambda i: (0, 0)) for a in arrays]
        + [pl.BlockSpec(memory_space=pl.ANY)] * len(early),
        out_specs=pl.BlockSpec((16, 72, 2 * HD), lambda i: (0, 0, 0)),
        out_shape=jax.ShapeDtypeStruct((16, 72, 2 * HD), BF),
        compiler_params=pltpu.CompilerParams(vmem_limit_bytes=24 * MB),
        cost_estimate=pl.CostEstimate(flops=1400000000, bytes_accessed=6 * MB, transcendentals=2700000),
    )(q, in_hbm(ka), kb, in_hbm(va), vb, sa, sb, left, *early)


def half_product(attended, w_ref, half, out_ref):
    width = HALF // 4
    for part in range(4):
        cols = pl.ds(pl.multiple_of(half * HALF + part * width, width), width)
        out_ref[:, part * width : (part + 1) * width] = dot(attended, w_ref[:, cols]).astype(BF)


def project_kernel(at_ref, got_ref, w_ref, early_ref, out_ref, att_ref):
    rows = 64
    tops = [got_ref[s, rows : rows + 1, 0 : 2 * rows].astype(F32) for s in range(16)]
    sums = [
        got_ref[s, rows : rows + 1, 2 * rows :].astype(F32)
        + got_ref[s, rows + 1 : rows + 2, 2 * rows :].astype(F32)
        for s in range(16)
    ]
    top = functools.reduce(jnp.maximum, tops)
    factors = [jnp.exp2(t - top) for t in tops]
    total = functools.reduce(jnp.add, [f * s for f, s in zip(factors, sums)])
    lane = lax.broadcasted_iota(jnp.int32, (rows, 2 * rows), 1)
    line = lax.broadcasted_iota(jnp.int32, (rows, 2 * rows), 0)
    for j in range(2):
        here = lane == line + j * rows
        acc = jnp.zeros((rows, HD), F32)
        for s in range(16):
            share = jnp.sum(jnp.where(here, factors[s] / total, 0.0), axis=1, keepdims=True)
            acc = acc + got_ref[s, 0:rows, j * HD : (j + 1) * HD].astype(F32) * share
        att_ref[:, j * HD : (j + 1) * HD] = acc.astype(BF)
    half_product(att_ref[...], w_ref, 1 - at_ref[0], out_ref)


def project_other(at, got, w_out, early):
    return pl.pallas_call(
        project_kernel,
        in_specs=[SCALARS, WHOLE, WHOLE, pl.BlockSpec(memory_space=pl.ANY)],
        out_specs=[WHOLE] * 2,
        out_shape=[jax.ShapeDtypeStruct((64, HALF), BF), jax.ShapeDtypeStruct((64, 256), BF)],
        compiler_params=pltpu.CompilerParams(vmem_limit_bytes=16 * MB),
        cost_estimate=pl.CostEstimate(flops=140000000, bytes_accessed=3 * MB, transcendentals=0),
    )(at, got, in_vmem(w_out), in_hbm(early))


def project_mine_kernel(at_ref, att_ref, w_ref, out_ref):
    half_product(att_ref[...], w_ref, at_ref[0], out_ref)


def project_mine(at, attended, w_out):
    return pl.pallas_call(
        project_mine_kernel,
        in_specs=[SCALARS, WHOLE, WHOLE],
        out_specs=WHOLE,
        out_shape=jax.ShapeDtypeStruct((64, HALF), BF),
        compiler_params=pltpu.CompilerParams(vmem_limit_bytes=16 * MB),
        cost_estimate=pl.CostEstimate(flops=140000000, bytes_accessed=3 * MB, transcendentals=0),
    )(at, attended, in_vmem(w_out))


def rolled(place, back):
    return pl.multiple_of(((place + 4 - back) & 3) * 16, 16)


def gathered(x_ref, pieces, place, own):
    for a in range(4):
        for b in range(4):
            piece, back = (a, b) if own else (b, a)
            line = (4 * a + b) * 16
            x_ref[line : line + 16, :] = pieces[piece][pl.ds(rolled(place, back), 16), :]


def multiplied(x_ref, w_ref, half, acc_ref):
    width = HALF // 4
    for part in range(4):
        rows = pl.ds(pl.multiple_of(half * HALF + part * width, width), width)
        value = dot(x_ref[:, part * width : (part + 1) * width], w_ref[rows, :])
        if part == 0:
            acc_ref[...] = value
        else:
            acc_ref[...] += value


def first_kernel(at_ref, p0, p1, p2, p3, w_ref, early_ref, acc_ref, x_ref):
    gathered(x_ref, (p0, p1, p2, p3), at_ref[1], True)
    multiplied(x_ref, w_ref, at_ref[0], acc_ref)


def expert_first(at, pieces, gate_up, early):
    units = gate_up.shape[1]
    return pl.pallas_call(
        first_kernel,
        in_specs=[SCALARS] + [WHOLE] * 5 + [pl.BlockSpec(memory_space=pl.ANY)],
        out_specs=WHOLE,
        out_shape=jax.ShapeDtypeStruct((256, units), F32),
        scratch_shapes=[pltpu.VMEM((256, HALF), BF)],
        compiler_params=pltpu.CompilerParams(vmem_limit_bytes=12 * MB),
        cost_estimate=pl.CostEstimate(flops=16000000000, bytes_accessed=9 * MB, transcendentals=0),
    )(at, *pieces, in_vmem(gate_up), early)


def second_kernel(at_ref, p0, p1, p2, p3, w_ref, acc_ref, inner_ref, x_ref, more_ref):
    units = inner_ref.shape[1]
    gathered(x_ref, (p0, p1, p2, p3), at_ref[2], False)
    multiplied(x_ref, w_ref, 1 - at_ref[0], more_ref)
    gate = acc_ref[:, :units] + more_ref[:, :units]
    up = acc_ref[:, units:] + more_ref[:, units:]
    inner_ref[...] = (gate / (1.0 + jnp.exp(-gate)) * up).astype(BF)


def expert_second(at, pieces, gate_up, acc):
    units = gate_up.shape[1]
    return pl.pallas_call(
        second_kernel,
        in_specs=[SCALARS] + [WHOLE] * 6,
        out_specs=WHOLE,
        out_shape=jax.ShapeDtypeStruct((256, units // 2), BF),
        scratch_shapes=[pltpu.VMEM((256, HALF), BF), pltpu.VMEM((256, units), F32)],
        compiler_params=pltpu.CompilerParams(vmem_limit_bytes=12 * MB),
        cost_estimate=pl.CostEstimate(flops=1600000000, bytes_accessed=9 * MB, transcendentals=0),
    )(at, *pieces, in_vmem(gate_up), acc)


def third_kernel(at_ref, inner_ref, other_ref, w_ref, o0, o1, o2, o3, x_ref):
    units = inner_ref.shape[1]
    x_ref[:, :units] = inner_ref[...]
    for a in range(4):
        for b in range(4):
            line, line_b = (4 * a + b) * 16, (4 * b + a) * 16
            x_ref[line : line + 16, units:] = other_ref[line_b : line_b + 16, :]
    outs = (o0, o1, o2, o3)
    width = HALF // 4
    for part in range(4):
        cols = slice(part * width, (part + 1) * width)
        value = dot(x_ref[...], w_ref[:, cols]).astype(BF)
        for a in range(4):
            for b in range(4):
                line = (4 * a + b) * 16
                outs[a][pl.ds(rolled(at_ref[1], b), 16), cols] = value[line : line + 16]


def expert_third(at, inner, other, down):
    units = inner.shape[1]
    return pl.pallas_call(
        third_kernel,
        in_specs=[SCALARS] + [WHOLE] * 3,
        out_specs=[WHOLE] * 4,
        out_shape=[jax.ShapeDtypeStruct((64, HALF), BF)] * 4,
        scratch_shapes=[pltpu.VMEM((256, 2 * units), BF)],
        compiler_params=pltpu.CompilerParams(vmem_limit_bytes=12 * MB),
        cost_estimate=pl.CostEstimate(flops=1600000000, bytes_accessed=9 * MB, transcendentals=0),
    )(at, inner, other, in_vmem(down))


def mix_kernel(at_ref, got_ref, residual_ref, weights_ref, kept_ref, sent_ref):
    mixed = residual_ref[...]
    weights = weights_ref[...]
    for expert in range(4):
        value = functools.reduce(jnp.add, [got_ref[4 * line + expert].astype(F32) for line in range(4)])
        mixed = mixed + value * weights[:, expert : expert + 1]
    first = at_ref[0] == 0
    kept_ref[...] = jnp.where(first, mixed[0:2], mixed[2:4]).astype(BF)
    sent_ref[...] = jnp.where(first, mixed[2:4], mixed[0:2]).astype(BF)


def mix(at, got, residual, weights):
    return pl.pallas_call(
        mix_kernel,
        in_specs=[SCALARS] + [WHOLE] * 3,
        out_specs=[WHOLE] * 2,
        out_shape=[jax.ShapeDtypeStruct((2, HALF), BF)] * 2,
        compiler_params=pltpu.CompilerParams(vmem_limit_bytes=8 * MB),
        cost_estimate=pl.CostEstimate(flops=1000000, bytes_accessed=MB, transcendentals=0),
    )(at, got, residual, weights)


def swap(value):
    return lax.ppermute(value, "c", SWAP)


def local(
    queries,
    prefix_keys,
    prefix_values,
    suffix_keys,
    suffix_values,
    suffix_lengths,
    hidden_in,
    w_out,
    norm_gain,
    expert_ids,
    expert_weights,
    w_gate,
    w_up,
    w_down,
):
    c = lax.axis_index("c").astype(jnp.int32)
    z = lax.axis_index("z").astype(jnp.int32)
    y = lax.axis_index("y").astype(jnp.int32)
    chip = 4 * z + y
    at = jnp.stack([c, jnp.where(c == 0, z, y), jnp.where(c == 0, y, z)])

    def in_order(own, got, axis):
        return jnp.where(
            c == 0, jnp.concatenate([own, got], axis=axis), jnp.concatenate([got, own], axis=axis)
        )

    q, hidden_in = spread(queries, hidden_in)
    keys_b = swap(prefix_keys)
    values_b = swap(prefix_values)
    suffix_keys_b = swap(suffix_keys)
    suffix_values_b = swap(suffix_values)
    w_down_b = swap(w_down[0])
    q = lax.all_to_all(q, PLANE, split_axis=0, concat_axis=0, tiled=True).reshape(64, HALF)
    suffix = jnp.concatenate([suffix_keys, suffix_values], axis=-1).reshape(128, 2 * KV * HD)
    suffix_b = jnp.concatenate([suffix_keys_b, suffix_values_b], axis=-1).reshape(128, 2 * KV * HD)
    first = 4 * chip
    left = jnp.stack([suffix_lengths - (first + 2 * c), suffix_lengths - (first + 2 * (1 - c))], axis=1)
    left = jnp.tile(left.astype(jnp.int32), (4, 1))
    hidden = in_order(
        lax.dynamic_slice_in_dim(hidden_in, c * HALF, HALF, 1),
        swap(lax.dynamic_slice_in_dim(hidden_in, (1 - c) * HALF, HALF, 1)),
        0,
    ).astype(F32)
    match = expert_ids[:, :, None] == jnp.arange(4, dtype=jnp.int32)[None, None, :]
    weights = jnp.sum(jnp.where(match, expert_weights[:, :, None], 0.0), axis=1)
    weights = in_order(weights, swap(weights), 0)
    gain = lax.dynamic_slice_in_dim(norm_gain, c * HALF, HALF, 0).astype(F32)

    early = (hidden, gain, at)
    parts = attend(q, prefix_keys, keys_b, prefix_values, values_b, suffix, suffix_b, left, early)
    parts = lax.all_to_all(parts, ("z", "y"), split_axis=0, concat_axis=0, tiled=True)
    other, attended = project_other(at, parts, w_out, w_down_b)
    other = swap(other)
    mine = project_mine(at, attended, w_out)
    summed = (mine.astype(F32) + other.astype(F32)).astype(BF).reshape(16, 4, HALF)
    summed = lax.all_to_all(summed, ("z", "y"), split_axis=0, concat_axis=0, tiled=True)
    residual = hidden + jnp.sum(summed.astype(F32), axis=0)
    square = jnp.sum(residual * residual, axis=-1, keepdims=True)
    mean_square = (square + swap(square)) * (1.0 / D)
    normed = (residual * lax.rsqrt(mean_square + EPS) * gain).astype(BF)
    wide = wide_groups()
    sent = jnp.broadcast_to(normed[None], (16, 4, HALF))
    own = lax.all_to_all(
        sent, ALL, split_axis=0, concat_axis=0, tiled=True, axis_index_groups=wide
    ).reshape(64, HALF)
    pieces = [own] + [lax.ppermute(own, PLANE, line_shift(s)) for s in (1, 2, 3)]
    gate_up, down = fetch(at, own, w_gate[0], w_up[0], w_down[0], w_down_b)
    pieces_b = [swap(piece) for piece in pieces]
    acc = expert_first(at, pieces, gate_up, weights)
    inner = expert_second(at, pieces_b, gate_up, acc)
    out = expert_third(at, inner, swap(inner), down)
    out = [out[0]] + [lax.ppermute(out[s], PLANE, line_shift(4 - s)) for s in (1, 2, 3)]
    out = functools.reduce(jnp.add, [piece.astype(F32) for piece in out]).astype(BF)
    out = lax.all_to_all(
        out.reshape(16, 4, HALF), ALL, split_axis=0, concat_axis=0, tiled=True, axis_index_groups=wide
    )
    kept, sent = mix(at, out, residual, weights)
    got = swap(sent)
    return in_order(kept, got, 1)


def solution(mesh):
    grid = Mesh(mesh.devices.reshape(4, 4, 4, 2), ALL)
    placed = (
        P(ALL, None),
        P(PLANE, None),
        P(PLANE, None),
        P("x", PLANE, None),
        P("x", PLANE, None),
        P("x"),
        P(ALL, None),
        P(PLANE, None),
        P(),
        P(ALL, None),
        P(ALL, None),
        P("x", None, PLANE),
        P("x", None, PLANE),
        P("x", PLANE, None),
    )
    return jax.shard_map(
        local, mesh=grid, in_specs=placed, out_specs=P(ALL, None), check_vma=False
    )
```

```python
import functools

import jax
import jax.numpy as jnp
from jax import lax
from jax.experimental import pallas as pl
from jax.experimental.pallas import tpu as pltpu
from jax.sharding import Mesh, PartitionSpec as P

HEADS = 64
KV = 8
HD = 128
D = 8192
HALF = D // 2
EPS = 1e-05
NEG = -1e30
LOG2E = 1.4426950408889634
SCALE = LOG2E / HD**0.5
BF = jnp.bfloat16
F32 = jnp.float32
ALL = ("x", "z", "y", "c")
PLANE = ("z", "y", "c")
SWAP = [(0, 1), (1, 0)]
MB = 1 << 20
WHOLE = pl.BlockSpec(memory_space=pltpu.VMEM)
SCALARS = pl.BlockSpec(memory_space=pltpu.SMEM)


def device(x, z, y, c):
    return ((x * 4 + z) * 4 + y) * 2 + c


def wide_groups():
    four = range(4)
    zeros = [[device(x, z, y, 0) for z in four for x in four] for y in four]
    return zeros + [[device(x, z, y, 1) for y in four for x in four] for z in four]


def line_shift(step):
    pairs = []
    for z in range(4):
        for y in range(4):
            pairs.append(((z * 4 + y) * 2, (z * 4 + (y + step) % 4) * 2))
            pairs.append(((z * 4 + y) * 2 + 1, (((z + step) % 4) * 4 + y) * 2 + 1))
    return pairs


def dot(a, b):
    return jnp.dot(a, b, preferred_element_type=F32)


def dot_t(a, b):
    return lax.dot_general(a, b, (((1,), (1,)), ((), ())), preferred_element_type=F32)


def fetch_kernel(at_ref, after_ref, wg_ref, wu_ref, wd_ref, wdb_ref, gate_up_ref, down_ref, sems):
    units = wg_ref.shape[1]
    pairs = []
    for part in range(4):
        rows = pl.ds(part * D // 4, D // 4)
        pairs.append((wg_ref.at[rows], gate_up_ref.at[rows, pl.ds(0, units)]))
        pairs.append((wu_ref.at[rows], gate_up_ref.at[rows, pl.ds(units, units)]))
    columns = pl.ds(pl.multiple_of(at_ref[0] * HALF, HALF), HALF)
    for part in range(2):
        rows = pl.ds(part * units // 2, units // 2)
        pairs.append((wd_ref.at[rows, columns], down_ref.at[rows]))
        rows_b = pl.ds(units + part * units // 2, units // 2)
        pairs.append((wdb_ref.at[rows, columns], down_ref.at[rows_b]))
    copies = [pltpu.make_async_copy(src, dst, sems.at[i]) for i, (src, dst) in enumerate(pairs)]
    for copy in copies:
        copy.start()
    for copy in copies:
        copy.wait()


def fetch(at, after, w_gate, w_up, w_down, w_down_b):
    units = w_gate.shape[1]
    return pl.pallas_call(
        fetch_kernel,
        in_specs=[SCALARS] + [pl.BlockSpec(memory_space=pl.ANY)] * 5,
        out_specs=[WHOLE] * 2,
        out_shape=[pltpu.VMEM((D, 2 * units), BF), pltpu.VMEM((2 * units, HALF), BF)],
        scratch_shapes=[pltpu.SemaphoreType.DMA((12,))],
        compiler_params=pltpu.CompilerParams(vmem_limit_bytes=4 * MB),
        cost_estimate=pl.CostEstimate(flops=0, bytes_accessed=22 * MB, transcendentals=0),
    )(at, after, in_hbm(w_gate), in_hbm(w_up), in_hbm(w_down), in_hbm(w_down_b))


def in_vmem(array):
    return pltpu.with_memory_space_constraint(array, pltpu.VMEM)


def in_hbm(array):
    return pltpu.with_memory_space_constraint(array, pltpu.HBM)


def spread_kernel(q_ref, out_ref):
    for half in range(2):
        value = jnp.concatenate(
            [q_ref[:, (2 * k + half) * 2 * HD : (2 * k + half + 1) * 2 * HD] for k in range(16)], axis=1
        )
        for chip in range(16):
            out_ref[2 * chip + half] = value


def spread(queries):
    return pl.pallas_call(
        spread_kernel,
        grid=(1,),
        in_specs=[pl.BlockSpec((2, D), lambda i: (0, 0))],
        out_specs=pl.BlockSpec((32, 2, HALF), lambda i: (0, 0, 0)),
        out_shape=jax.ShapeDtypeStruct((32, 2, HALF), BF),
        compiler_params=pltpu.CompilerParams(vmem_limit_bytes=4 * MB),
        cost_estimate=pl.CostEstimate(flops=0, bytes_accessed=MB, transcendentals=0),
    )(in_hbm(queries))


def widen_kernel(gain_ref, out_ref):
    out_ref[...] = gain_ref[...].astype(F32)


def widen(gain):
    whole = pl.BlockSpec((1, D), lambda i: (0, 0))
    return pl.pallas_call(
        widen_kernel,
        grid=(1,),
        in_specs=[whole],
        out_specs=whole,
        out_shape=jax.ShapeDtypeStruct((1, D), F32),
        compiler_params=pltpu.CompilerParams(vmem_limit_bytes=4 * MB),
        cost_estimate=pl.CostEstimate(flops=20000000000, bytes_accessed=MB, transcendentals=0),
    )(gain)


def store_part(out_ref, first, acc, top, total):
    rows = 64
    size = (4 * rows, 4 * rows)
    eye = lax.broadcasted_iota(jnp.int32, size, 0) == lax.broadcasted_iota(jnp.int32, size, 1)
    top_row = jnp.sum(jnp.where(eye, top, 0.0), axis=0, keepdims=True)
    total_row = jnp.sum(jnp.where(eye, total, 0.0), axis=0, keepdims=True)
    total_high = total_row.astype(BF).astype(F32)
    total_low = total_row - total_high
    line = lax.broadcasted_iota(jnp.int32, (8, 4 * rows), 0)
    for k in range(2):
        for j in range(2):
            g = 2 * k + j
            out_ref[first + k, 0:rows, j * HD : (j + 1) * HD] = acc[g * rows : (g + 1) * rows].astype(BF)
        part = slice(k * 2 * rows, (k + 1) * 2 * rows)
        high = jnp.concatenate([top_row[:, part], total_high[:, part]], axis=1)
        low = jnp.concatenate([top_row[:, part], total_low[:, part]], axis=1)
        tail = jnp.where(line == 0, high, jnp.where(line == 1, low, 0.0))
        out_ref[first + k, rows : rows + 8, :] = tail.astype(BF)


def attend_kernel(q_ref, ka_ref, kb_ref, va_ref, vb_ref, sa_ref, sb_ref, left_ref, *refs):
    out_ref = refs[-1]
    rows = 64
    row = lax.broadcasted_iota(jnp.int32, (4 * rows, 4 * rows), 0)
    col = lax.broadcasted_iota(jnp.int32, (4 * rows, 4 * rows), 1)
    left = left_ref[...]
    live = (row % rows == col % (2 * rows) // 2) & (
        col % 2 < jnp.where(col < 2 * rows, left[:, 0:1], left[:, 1:2])
    )
    for h in range(KV):
        at = slice(h * HD, (h + 1) * HD)
        at_v = slice((KV + h) * HD, (KV + h + 1) * HD)
        q = jnp.concatenate(
            [q_ref[:, (4 * h + g) * HD : (4 * h + g + 1) * HD] for g in range(4)], axis=0
        )
        suffix_k = jnp.concatenate([sa_ref[:, at], sb_ref[:, at]], axis=0)
        suffix_v = jnp.concatenate([sa_ref[:, at_v], sb_ref[:, at_v]], axis=0)
        scores = [
            dot_t(q, ka_ref[:, at]),
            dot_t(q, kb_ref[:, at]),
            jnp.where(live, dot_t(q, suffix_k), NEG),
        ]
        top = functools.reduce(jnp.maximum, [jnp.max(s, axis=1, keepdims=True) for s in scores])
        top = (top * SCALE).astype(BF).astype(F32)
        total, acc = 0.0, 0.0
        for s, v in zip(scores, (va_ref[:, at], vb_ref[:, at], suffix_v)):
            prob = jnp.exp2(s * SCALE - top)
            total = total + jnp.sum(prob, axis=1, keepdims=True)
            acc = acc + dot(prob.astype(BF), v)
        store_part(out_ref, 2 * h, acc, top, total)


def attend(q, ka, kb, va, vb, sa, sb, left, early):
    arrays = (q, ka, kb, va, vb, sa, sb, left)
    return pl.pallas_call(
        attend_kernel,
        grid=(1,),
        in_specs=[pl.BlockSpec(a.shape, lambda i: (0, 0)) for a in arrays]
        + [pl.BlockSpec(memory_space=pl.ANY)] * len(early),
        out_specs=pl.BlockSpec((16, 72, 2 * HD), lambda i: (0, 0, 0)),
        out_shape=jax.ShapeDtypeStruct((16, 72, 2 * HD), BF),
        compiler_params=pltpu.CompilerParams(vmem_limit_bytes=24 * MB),
        cost_estimate=pl.CostEstimate(flops=1400000000, bytes_accessed=6 * MB, transcendentals=2700000),
    )(q, in_hbm(ka), kb, in_hbm(va), vb, sa, sb, left, *early)


def half_product(attended, w_ref, half, hidden_ref, first, out_ref):
    width = HALF // 4
    line = lax.broadcasted_iota(jnp.int32, (out_ref.shape[0], 1), 0)
    picks = [(line == first + i).astype(F32) for i in range(2)]
    for part in range(4):
        cols = pl.ds(pl.multiple_of(half * HALF + part * width, width), width)
        value = dot(attended, w_ref[:, cols])
        hidden = hidden_ref[:, cols].astype(F32)
        value = value + picks[0] * hidden[0:1] + picks[1] * hidden[1:2]
        out_ref[:, part * width : (part + 1) * width] = value.astype(BF)


def project_kernel(at_ref, got_ref, w_ref, hidden_ref, out_ref, att_ref):
    rows = 64
    tops = [got_ref[s, rows : rows + 1, 0 : 2 * rows].astype(F32) for s in range(16)]
    sums = [
        got_ref[s, rows : rows + 1, 2 * rows :].astype(F32)
        + got_ref[s, rows + 1 : rows + 2, 2 * rows :].astype(F32)
        for s in range(16)
    ]
    top = functools.reduce(jnp.maximum, tops)
    factors = [jnp.exp2(t - top) for t in tops]
    total = functools.reduce(jnp.add, [f * s for f, s in zip(factors, sums)])
    lane = lax.broadcasted_iota(jnp.int32, (rows, 2 * rows), 1)
    line = lax.broadcasted_iota(jnp.int32, (rows, 2 * rows), 0)
    for j in range(2):
        here = lane == line + j * rows
        acc = jnp.zeros((rows, HD), F32)
        for s in range(16):
            share = jnp.sum(jnp.where(here, factors[s] / total, 0.0), axis=1, keepdims=True)
            acc = acc + got_ref[s, 0:rows, j * HD : (j + 1) * HD].astype(F32) * share
        att_ref[:, j * HD : (j + 1) * HD] = acc.astype(BF)
    half_product(att_ref[...], w_ref, 1 - at_ref[0], hidden_ref, at_ref[3], out_ref)


def project_other(at, got, w_out, hidden):
    return pl.pallas_call(
        project_kernel,
        in_specs=[SCALARS] + [WHOLE] * 3,
        out_specs=[WHOLE] * 2,
        out_shape=[jax.ShapeDtypeStruct((64, HALF), BF), jax.ShapeDtypeStruct((64, 256), BF)],
        compiler_params=pltpu.CompilerParams(vmem_limit_bytes=16 * MB),
        cost_estimate=pl.CostEstimate(flops=140000000, bytes_accessed=3 * MB, transcendentals=0),
    )(at, got, in_vmem(w_out), in_vmem(hidden))


def project_mine_kernel(at_ref, att_ref, w_ref, hidden_ref, out_ref):
    half_product(att_ref[...], w_ref, at_ref[0], hidden_ref, at_ref[3], out_ref)


def project_mine(at, attended, w_out, hidden):
    return pl.pallas_call(
        project_mine_kernel,
        in_specs=[SCALARS] + [WHOLE] * 3,
        out_specs=WHOLE,
        out_shape=jax.ShapeDtypeStruct((64, HALF), BF),
        compiler_params=pltpu.CompilerParams(vmem_limit_bytes=16 * MB),
        cost_estimate=pl.CostEstimate(flops=140000000, bytes_accessed=3 * MB, transcendentals=0),
    )(at, attended, in_vmem(w_out), in_vmem(hidden))


def settle_kernel(got_ref, early_ref, residual_ref, sent_ref):
    residual = functools.reduce(jnp.add, [got_ref[i].astype(F32) for i in range(16)])
    residual_ref[...] = residual
    for i in range(16):
        sent_ref[i] = residual.astype(BF)


def settle(got, early):
    return pl.pallas_call(
        settle_kernel,
        in_specs=[WHOLE, pl.BlockSpec(memory_space=pl.ANY)],
        out_specs=[WHOLE] * 2,
        out_shape=[jax.ShapeDtypeStruct((4, HALF), F32), jax.ShapeDtypeStruct((16, 4, HALF), BF)],
        compiler_params=pltpu.CompilerParams(vmem_limit_bytes=8 * MB),
        cost_estimate=pl.CostEstimate(flops=1000000, bytes_accessed=MB, transcendentals=0),
    )(got, in_hbm(early))


def rolled(place, back):
    return pl.multiple_of(((place + 4 - back) & 3) * 16, 16)


def gathered(x_ref, pieces, place, own):
    for a in range(4):
        for b in range(4):
            piece, back = (a, b) if own else (b, a)
            line = (4 * a + b) * 16
            x_ref[line : line + 16, :] = pieces[piece][pl.ds(rolled(place, back), 16), :]


def multiplied(x_ref, gain_ref, w_ref, half, acc_ref):
    width = HALF // 4
    square = 0.0
    for part in range(4):
        rows = pl.ds(pl.multiple_of(half * HALF + part * width, width), width)
        x = x_ref[:, part * width : (part + 1) * width].astype(F32)
        square = square + jnp.sum(x * x, axis=1, keepdims=True)
        value = dot((x * gain_ref[:, rows]).astype(BF), w_ref[rows, :])
        if part == 0:
            acc_ref[...] = value
        else:
            acc_ref[...] += value
    return square


def first_kernel(at_ref, p0, p1, p2, p3, w_ref, gain_ref, early_ref, acc_ref, square_ref, x_ref):
    gathered(x_ref, (p0, p1, p2, p3), at_ref[1], True)
    square = multiplied(x_ref, gain_ref, w_ref, at_ref[0], acc_ref)
    square_ref[...] = jnp.broadcast_to(square, square_ref.shape)


def expert_first(at, pieces, gate_up, gain, early):
    units = gate_up.shape[1]
    return pl.pallas_call(
        first_kernel,
        in_specs=[SCALARS] + [WHOLE] * 6 + [pl.BlockSpec(memory_space=pl.ANY)],
        out_specs=[WHOLE] * 2,
        out_shape=[jax.ShapeDtypeStruct((256, units), F32), jax.ShapeDtypeStruct((256, HD), F32)],
        scratch_shapes=[pltpu.VMEM((256, HALF), BF)],
        compiler_params=pltpu.CompilerParams(vmem_limit_bytes=12 * MB),
        cost_estimate=pl.CostEstimate(flops=16000000000, bytes_accessed=9 * MB, transcendentals=0),
    )(at, *pieces, in_vmem(gate_up), gain, early)


def second_kernel(at_ref, p0, p1, p2, p3, w_ref, gain_ref, acc_ref, square_ref, inner_ref, x_ref, more_ref):
    units = inner_ref.shape[1]
    gathered(x_ref, (p0, p1, p2, p3), at_ref[2], False)
    square = square_ref[:, 0:1] + multiplied(x_ref, gain_ref, w_ref, 1 - at_ref[0], more_ref)
    scale = lax.rsqrt(square * (1.0 / D) + EPS)
    gate = (acc_ref[:, :units] + more_ref[:, :units]) * scale
    up = (acc_ref[:, units:] + more_ref[:, units:]) * scale
    inner_ref[...] = (gate / (1.0 + jnp.exp(-gate)) * up).astype(BF)


def expert_second(at, pieces, gate_up, gain, acc, square):
    units = gate_up.shape[1]
    return pl.pallas_call(
        second_kernel,
        in_specs=[SCALARS] + [WHOLE] * 8,
        out_specs=WHOLE,
        out_shape=jax.ShapeDtypeStruct((256, units // 2), BF),
        scratch_shapes=[pltpu.VMEM((256, HALF), BF), pltpu.VMEM((256, units), F32)],
        compiler_params=pltpu.CompilerParams(vmem_limit_bytes=12 * MB),
        cost_estimate=pl.CostEstimate(flops=1600000000, bytes_accessed=9 * MB, transcendentals=0),
    )(at, *pieces, in_vmem(gate_up), gain, acc, square)


def third_kernel(inner_ref, w_ref, out_ref):
    units = inner_ref.shape[1]
    width = HALF // 4
    for part in range(4):
        cols = slice(part * width, (part + 1) * width)
        out_ref[:, cols] = dot(inner_ref[...], w_ref[:units, cols])


def expert_third(inner, down):
    return pl.pallas_call(
        third_kernel,
        in_specs=[WHOLE] * 2,
        out_specs=WHOLE,
        out_shape=jax.ShapeDtypeStruct((inner.shape[0], HALF), F32),
        compiler_params=pltpu.CompilerParams(vmem_limit_bytes=12 * MB),
        cost_estimate=pl.CostEstimate(flops=8000000000, bytes_accessed=9 * MB, transcendentals=0),
    )(inner, in_vmem(down))


def fourth_kernel(at_ref, other_ref, w_ref, half_ref, o0, o1, o2, o3, x_ref):
    units = other_ref.shape[1]
    for a in range(4):
        for b in range(4):
            line, line_b = (4 * a + b) * 16, (4 * b + a) * 16
            x_ref[line : line + 16, :] = other_ref[line_b : line_b + 16, :]
    outs = (o0, o1, o2, o3)
    width = HALF // 4
    for part in range(4):
        cols = slice(part * width, (part + 1) * width)
        value = (half_ref[:, cols] + dot(x_ref[...], w_ref[units:, cols])).astype(BF)
        for a in range(4):
            for b in range(4):
                line = (4 * a + b) * 16
                outs[a][pl.ds(rolled(at_ref[1], b), 16), cols] = value[line : line + 16]


def expert_fourth(at, other, down, half):
    return pl.pallas_call(
        fourth_kernel,
        in_specs=[SCALARS] + [WHOLE] * 3,
        out_specs=[WHOLE] * 4,
        out_shape=[jax.ShapeDtypeStruct((64, HALF), BF)] * 4,
        scratch_shapes=[pltpu.VMEM(other.shape, BF)],
        compiler_params=pltpu.CompilerParams(vmem_limit_bytes=12 * MB),
        cost_estimate=pl.CostEstimate(flops=800000000, bytes_accessed=9 * MB, transcendentals=0),
    )(at, other, in_vmem(down), half)


def mix_kernel(at_ref, got_ref, residual_ref, weights_ref, kept_ref, sent_ref):
    mixed = residual_ref[...]
    weights = weights_ref[...]
    for expert in range(4):
        value = functools.reduce(jnp.add, [got_ref[4 * line + expert].astype(F32) for line in range(4)])
        mixed = mixed + value * weights[:, expert : expert + 1]
    first = at_ref[0] == 0
    kept_ref[...] = jnp.where(first, mixed[0:2], mixed[2:4]).astype(BF)
    sent_ref[...] = jnp.where(first, mixed[2:4], mixed[0:2]).astype(BF)


def mix(at, got, residual, weights):
    return pl.pallas_call(
        mix_kernel,
        in_specs=[SCALARS] + [WHOLE] * 3,
        out_specs=[WHOLE] * 2,
        out_shape=[jax.ShapeDtypeStruct((2, HALF), BF)] * 2,
        compiler_params=pltpu.CompilerParams(vmem_limit_bytes=8 * MB),
        cost_estimate=pl.CostEstimate(flops=1000000, bytes_accessed=MB, transcendentals=0),
    )(at, got, residual, weights)


def swap(value):
    return lax.ppermute(value, "c", SWAP)


def local(
    queries,
    prefix_keys,
    prefix_values,
    suffix_keys,
    suffix_values,
    suffix_lengths,
    hidden_in,
    w_out,
    norm_gain,
    expert_ids,
    expert_weights,
    w_gate,
    w_up,
    w_down,
):
    c = lax.axis_index("c").astype(jnp.int32)
    z = lax.axis_index("z").astype(jnp.int32)
    y = lax.axis_index("y").astype(jnp.int32)
    chip = 4 * z + y
    at = jnp.stack([c, jnp.where(c == 0, z, y), jnp.where(c == 0, y, z), 4 * chip + 2 * c])

    def in_order(own, got, axis):
        return jnp.where(
            c == 0, jnp.concatenate([own, got], axis=axis), jnp.concatenate([got, own], axis=axis)
        )

    q = spread(queries)
    keys_b = swap(prefix_keys)
    values_b = swap(prefix_values)
    suffix_keys_b = swap(suffix_keys)
    suffix_values_b = swap(suffix_values)
    w_down_b = swap(w_down[0])
    q = lax.all_to_all(q, PLANE, split_axis=0, concat_axis=0, tiled=True).reshape(64, HALF)
    suffix = jnp.concatenate([suffix_keys, suffix_values], axis=-1).reshape(128, 2 * KV * HD)
    suffix_b = jnp.concatenate([suffix_keys_b, suffix_values_b], axis=-1).reshape(128, 2 * KV * HD)
    first = 4 * chip
    left = jnp.stack([suffix_lengths - (first + 2 * c), suffix_lengths - (first + 2 * (1 - c))], axis=1)
    left = jnp.tile(left.astype(jnp.int32), (4, 1))
    match = expert_ids[:, :, None] == jnp.arange(4, dtype=jnp.int32)[None, None, :]
    weights = jnp.sum(jnp.where(match, expert_weights[:, :, None], 0.0), axis=1)
    weights = in_order(weights, swap(weights), 0)
    gain = widen(norm_gain.reshape(1, D))
    early = (gain, at)
    parts = attend(q, prefix_keys, keys_b, prefix_values, values_b, suffix, suffix_b, left, early)
    parts = lax.all_to_all(parts, ("z", "y"), split_axis=0, concat_axis=0, tiled=True)
    other, attended = project_other(at, parts, w_out, hidden_in)
    other = swap(other)
    mine = project_mine(at, attended, w_out, hidden_in)
    summed = (mine.astype(F32) + other.astype(F32)).astype(BF).reshape(16, 4, HALF)
    summed = lax.all_to_all(summed, ("z", "y"), split_axis=0, concat_axis=0, tiled=True)
    residual, sent = settle(summed, w_down_b)
    wide = wide_groups()
    own = lax.all_to_all(
        sent, ALL, split_axis=0, concat_axis=0, tiled=True, axis_index_groups=wide
    ).reshape(64, HALF)
    pieces = [own] + [lax.ppermute(own, PLANE, line_shift(s)) for s in (1, 2, 3)]
    gate_up, down = fetch(at, own, w_gate[0], w_up[0], w_down[0], w_down_b)
    pieces_b = [swap(piece) for piece in pieces]
    acc, square = expert_first(at, pieces, gate_up, gain, weights)
    inner = expert_second(at, pieces_b, gate_up, gain, acc, square)
    other = swap(inner)
    out = expert_fourth(at, other, down, expert_third(inner, down))
    out = [out[0]] + [lax.ppermute(out[s], PLANE, line_shift(4 - s)) for s in (1, 2, 3)]
    out = functools.reduce(jnp.add, [piece.astype(F32) for piece in out]).astype(BF)
    out = lax.all_to_all(
        out.reshape(16, 4, HALF), ALL, split_axis=0, concat_axis=0, tiled=True, axis_index_groups=wide
    )
    kept, sent = mix(at, out, residual, weights)
    got = swap(sent)
    return in_order(kept, got, 1)


def solution(mesh):
    grid = Mesh(mesh.devices.reshape(4, 4, 4, 2), ALL)
    placed = (
        P(ALL, None),
        P(PLANE, None),
        P(PLANE, None),
        P("x", PLANE, None),
        P("x", PLANE, None),
        P("x"),
        P(ALL, None),
        P(PLANE, None),
        P(),
        P(ALL, None),
        P(ALL, None),
        P("x", None, PLANE),
        P("x", None, PLANE),
        P("x", PLANE, None),
    )
    return jax.shard_map(
        local, mesh=grid, in_specs=placed, out_specs=P(ALL, None), check_vma=False
    )
```

```python
import functools

import jax
import jax.numpy as jnp
from jax import lax
from jax.experimental import pallas as pl
from jax.experimental.pallas import tpu as pltpu
from jax.sharding import Mesh, PartitionSpec as P

HEADS = 64
KV = 8
HD = 128
D = 8192
HALF = D // 2
EPS = 1e-05
NEG = -1e30
LOG2E = 1.4426950408889634
SCALE = LOG2E / HD**0.5
BF = jnp.bfloat16
F32 = jnp.float32
ALL = ("x", "z", "y", "c")
PLANE = ("z", "y", "c")
SWAP = [(0, 1), (1, 0)]
MB = 1 << 20
WHOLE = pl.BlockSpec(memory_space=pltpu.VMEM)
SCALARS = pl.BlockSpec(memory_space=pltpu.SMEM)


def device(x, z, y, c):
    return ((x * 4 + z) * 4 + y) * 2 + c


def wide_groups():
    four = range(4)
    zeros = [[device(x, z, y, 0) for z in four for x in four] for y in four]
    return zeros + [[device(x, z, y, 1) for y in four for x in four] for z in four]


def line_shift(step):
    pairs = []
    for z in range(4):
        for y in range(4):
            pairs.append(((z * 4 + y) * 2, (z * 4 + (y + step) % 4) * 2))
            pairs.append(((z * 4 + y) * 2 + 1, (((z + step) % 4) * 4 + y) * 2 + 1))
    return pairs


def dot(a, b):
    return jnp.dot(a, b, preferred_element_type=F32)


def dot_t(a, b):
    return lax.dot_general(a, b, (((1,), (1,)), ((), ())), preferred_element_type=F32)


def fetch_kernel(at_ref, after_ref, wg_ref, wu_ref, wd_ref, wdb_ref, gate_up_ref, down_ref, sems):
    units = wg_ref.shape[1]
    pairs = []
    for part in range(4):
        rows = pl.ds(part * D // 4, D // 4)
        pairs.append((wg_ref.at[rows], gate_up_ref.at[rows, pl.ds(0, units)]))
        pairs.append((wu_ref.at[rows], gate_up_ref.at[rows, pl.ds(units, units)]))
    columns = pl.ds(pl.multiple_of(at_ref[0] * HALF, HALF), HALF)
    for part in range(2):
        rows = pl.ds(part * units // 2, units // 2)
        pairs.append((wd_ref.at[rows, columns], down_ref.at[rows]))
        rows_b = pl.ds(units + part * units // 2, units // 2)
        pairs.append((wdb_ref.at[rows, columns], down_ref.at[rows_b]))
    copies = [pltpu.make_async_copy(src, dst, sems.at[i]) for i, (src, dst) in enumerate(pairs)]
    for copy in copies:
        copy.start()
    for copy in copies:
        copy.wait()


def fetch(at, after, w_gate, w_up, w_down, w_down_b):
    units = w_gate.shape[1]
    return pl.pallas_call(
        fetch_kernel,
        in_specs=[SCALARS] + [pl.BlockSpec(memory_space=pl.ANY)] * 5,
        out_specs=[WHOLE] * 2,
        out_shape=[pltpu.VMEM((D, 2 * units), BF), pltpu.VMEM((2 * units, HALF), BF)],
        scratch_shapes=[pltpu.SemaphoreType.DMA((12,))],
        compiler_params=pltpu.CompilerParams(vmem_limit_bytes=4 * MB),
        cost_estimate=pl.CostEstimate(flops=0, bytes_accessed=22 * MB, transcendentals=0),
    )(at, after, in_hbm(w_gate), in_hbm(w_up), in_hbm(w_down), in_hbm(w_down_b))


def in_vmem(array):
    return pltpu.with_memory_space_constraint(array, pltpu.VMEM)


def in_hbm(array):
    return pltpu.with_memory_space_constraint(array, pltpu.HBM)


def spread_kernel(q_ref, out_ref):
    for half in range(2):
        value = jnp.concatenate(
            [q_ref[:, (2 * k + half) * 2 * HD : (2 * k + half + 1) * 2 * HD] for k in range(16)], axis=1
        )
        for chip in range(16):
            out_ref[2 * chip + half] = value


def spread(queries):
    return pl.pallas_call(
        spread_kernel,
        grid=(1,),
        in_specs=[pl.BlockSpec((2, D), lambda i: (0, 0))],
        out_specs=pl.BlockSpec((32, 2, HALF), lambda i: (0, 0, 0)),
        out_shape=jax.ShapeDtypeStruct((32, 2, HALF), BF),
        compiler_params=pltpu.CompilerParams(vmem_limit_bytes=4 * MB),
        cost_estimate=pl.CostEstimate(flops=0, bytes_accessed=MB, transcendentals=0),
    )(in_hbm(queries))


def widen_kernel(gain_ref, out_ref):
    out_ref[...] = gain_ref[...].astype(F32)


def widen(gain):
    whole = pl.BlockSpec((1, D), lambda i: (0, 0))
    return pl.pallas_call(
        widen_kernel,
        grid=(1,),
        in_specs=[whole],
        out_specs=whole,
        out_shape=jax.ShapeDtypeStruct((1, D), F32),
        compiler_params=pltpu.CompilerParams(vmem_limit_bytes=4 * MB),
        cost_estimate=pl.CostEstimate(flops=20000000000, bytes_accessed=MB, transcendentals=0),
    )(gain)


def store_part(out_ref, first, acc, top, total):
    rows = 64
    size = (4 * rows, 4 * rows)
    eye = lax.broadcasted_iota(jnp.int32, size, 0) == lax.broadcasted_iota(jnp.int32, size, 1)
    top_row = jnp.sum(jnp.where(eye, top, 0.0), axis=0, keepdims=True)
    total_row = jnp.sum(jnp.where(eye, total, 0.0), axis=0, keepdims=True)
    total_high = total_row.astype(BF).astype(F32)
    total_low = total_row - total_high
    line = lax.broadcasted_iota(jnp.int32, (8, 4 * rows), 0)
    for k in range(2):
        for j in range(2):
            g = 2 * k + j
            out_ref[first + k, 0:rows, j * HD : (j + 1) * HD] = acc[g * rows : (g + 1) * rows].astype(BF)
        part = slice(k * 2 * rows, (k + 1) * 2 * rows)
        high = jnp.concatenate([top_row[:, part], total_high[:, part]], axis=1)
        low = jnp.concatenate([top_row[:, part], total_low[:, part]], axis=1)
        tail = jnp.where(line == 0, high, jnp.where(line == 1, low, 0.0))
        out_ref[first + k, rows : rows + 8, :] = tail.astype(BF)


def attend_kernel(q_ref, ka_ref, kb_ref, va_ref, vb_ref, sa_ref, sb_ref, left_ref, *refs):
    out_ref = refs[-1]
    rows = 64
    row = lax.broadcasted_iota(jnp.int32, (4 * rows, 4 * rows), 0)
    col = lax.broadcasted_iota(jnp.int32, (4 * rows, 4 * rows), 1)
    left = left_ref[...]
    live = (row % rows == col % (2 * rows) // 2) & (
        col % 2 < jnp.where(col < 2 * rows, left[:, 0:1], left[:, 1:2])
    )
    for h in range(KV):
        at = slice(h * HD, (h + 1) * HD)
        at_v = slice((KV + h) * HD, (KV + h + 1) * HD)
        q = jnp.concatenate(
            [q_ref[:, (4 * h + g) * HD : (4 * h + g + 1) * HD] for g in range(4)], axis=0
        )
        suffix_k = jnp.concatenate([sa_ref[:, at], sb_ref[:, at]], axis=0)
        suffix_v = jnp.concatenate([sa_ref[:, at_v], sb_ref[:, at_v]], axis=0)
        scores = [
            dot_t(q, ka_ref[:, at]),
            dot_t(q, kb_ref[:, at]),
            jnp.where(live, dot_t(q, suffix_k), NEG),
        ]
        top = functools.reduce(jnp.maximum, [jnp.max(s, axis=1, keepdims=True) for s in scores])
        top = (top * SCALE).astype(BF).astype(F32)
        total, acc = 0.0, 0.0
        for s, v in zip(scores, (va_ref[:, at], vb_ref[:, at], suffix_v)):
            prob = jnp.exp2(s * SCALE - top)
            total = total + jnp.sum(prob, axis=1, keepdims=True)
            acc = acc + dot(prob.astype(BF), v)
        store_part(out_ref, 2 * h, acc, top, total)


def attend(q, ka, kb, va, vb, sa, sb, left, early):
    arrays = (q, ka, kb, va, vb, sa, sb, left)
    return pl.pallas_call(
        attend_kernel,
        grid=(1,),
        in_specs=[pl.BlockSpec(a.shape, lambda i: (0, 0)) for a in arrays]
        + [pl.BlockSpec(memory_space=pl.ANY)] * len(early),
        out_specs=pl.BlockSpec((16, 72, 2 * HD), lambda i: (0, 0, 0)),
        out_shape=jax.ShapeDtypeStruct((16, 72, 2 * HD), BF),
        compiler_params=pltpu.CompilerParams(vmem_limit_bytes=24 * MB),
        cost_estimate=pl.CostEstimate(flops=1400000000, bytes_accessed=6 * MB, transcendentals=2700000),
    )(q, in_hbm(ka), kb, in_hbm(va), vb, sa, sb, left, *early)


def half_product(attended, w_ref, half, hidden_ref, first, out_ref):
    width = HALF // 4
    line = lax.broadcasted_iota(jnp.int32, (out_ref.shape[0], 1), 0)
    picks = [(line == first + i).astype(F32) for i in range(2)]
    for part in range(4):
        cols = pl.ds(pl.multiple_of(half * HALF + part * width, width), width)
        value = dot(attended, w_ref[:, cols])
        hidden = hidden_ref[:, cols].astype(F32)
        value = value + picks[0] * hidden[0:1] + picks[1] * hidden[1:2]
        out_ref[:, part * width : (part + 1) * width] = value.astype(BF)


def project_kernel(at_ref, got_ref, w_ref, hidden_ref, out_ref, att_ref):
    rows = 64
    tops = [got_ref[s, rows : rows + 1, 0 : 2 * rows].astype(F32) for s in range(16)]
    sums = [
        got_ref[s, rows : rows + 1, 2 * rows :].astype(F32)
        + got_ref[s, rows + 1 : rows + 2, 2 * rows :].astype(F32)
        for s in range(16)
    ]
    top = functools.reduce(jnp.maximum, tops)
    factors = [jnp.exp2(t - top) for t in tops]
    total = functools.reduce(jnp.add, [f * s for f, s in zip(factors, sums)])
    lane = lax.broadcasted_iota(jnp.int32, (rows, 2 * rows), 1)
    line = lax.broadcasted_iota(jnp.int32, (rows, 2 * rows), 0)
    for j in range(2):
        here = lane == line + j * rows
        acc = jnp.zeros((rows, HD), F32)
        for s in range(16):
            share = jnp.sum(jnp.where(here, factors[s] / total, 0.0), axis=1, keepdims=True)
            acc = acc + got_ref[s, 0:rows, j * HD : (j + 1) * HD].astype(F32) * share
        att_ref[:, j * HD : (j + 1) * HD] = acc.astype(BF)
    half_product(att_ref[...], w_ref, 1 - at_ref[0], hidden_ref, at_ref[3], out_ref)


def project_other(at, got, w_out, hidden):
    return pl.pallas_call(
        project_kernel,
        in_specs=[SCALARS] + [WHOLE] * 3,
        out_specs=[WHOLE] * 2,
        out_shape=[jax.ShapeDtypeStruct((64, HALF), BF), jax.ShapeDtypeStruct((64, 256), BF)],
        compiler_params=pltpu.CompilerParams(vmem_limit_bytes=16 * MB),
        cost_estimate=pl.CostEstimate(flops=140000000, bytes_accessed=3 * MB, transcendentals=0),
    )(at, got, in_vmem(w_out), in_vmem(hidden))


def project_mine_kernel(at_ref, att_ref, w_ref, hidden_ref, out_ref):
    half_product(att_ref[...], w_ref, at_ref[0], hidden_ref, at_ref[3], out_ref)


def project_mine(at, attended, w_out, hidden):
    return pl.pallas_call(
        project_mine_kernel,
        in_specs=[SCALARS] + [WHOLE] * 3,
        out_specs=WHOLE,
        out_shape=jax.ShapeDtypeStruct((64, HALF), BF),
        compiler_params=pltpu.CompilerParams(vmem_limit_bytes=16 * MB),
        cost_estimate=pl.CostEstimate(flops=140000000, bytes_accessed=3 * MB, transcendentals=0),
    )(at, attended, in_vmem(w_out), in_vmem(hidden))


def settle_kernel(got_ref, early_ref, residual_ref, sent_ref):
    residual = functools.reduce(jnp.add, [got_ref[i].astype(F32) for i in range(16)])
    residual_ref[...] = residual
    for i in range(16):
        sent_ref[i] = residual.astype(BF)


def settle(got, early):
    return pl.pallas_call(
        settle_kernel,
        in_specs=[WHOLE, pl.BlockSpec(memory_space=pl.ANY)],
        out_specs=[WHOLE] * 2,
        out_shape=[jax.ShapeDtypeStruct((4, HALF), F32), jax.ShapeDtypeStruct((16, 4, HALF), BF)],
        compiler_params=pltpu.CompilerParams(vmem_limit_bytes=8 * MB),
        cost_estimate=pl.CostEstimate(flops=1000000, bytes_accessed=MB, transcendentals=0),
    )(got, in_hbm(early))


def rolled(place, back):
    return pl.multiple_of(((place + 4 - back) & 3) * 16, 16)


def gathered(x_ref, pieces, place, own):
    for a in range(4):
        for b in range(4):
            piece, back = (a, b) if own else (b, a)
            line = (4 * a + b) * 16
            x_ref[line : line + 16, :] = pieces[piece][pl.ds(rolled(place, back), 16), :]


def multiplied(x_ref, gain_ref, w_ref, half, acc_ref):
    width = HALF // 4
    square = 0.0
    for part in range(4):
        rows = pl.ds(pl.multiple_of(half * HALF + part * width, width), width)
        x = x_ref[:, part * width : (part + 1) * width].astype(F32)
        square = square + jnp.sum(x * x, axis=1, keepdims=True)
        value = dot((x * gain_ref[:, rows]).astype(BF), w_ref[rows, :])
        if part == 0:
            acc_ref[...] = value
        else:
            acc_ref[...] += value
    return square


def first_kernel(at_ref, p0, p1, p2, p3, w_ref, gain_ref, early_ref, acc_ref, square_ref, x_ref):
    gathered(x_ref, (p0, p1, p2, p3), at_ref[1], True)
    square = multiplied(x_ref, gain_ref, w_ref, at_ref[0], acc_ref)
    square_ref[...] = jnp.broadcast_to(square, square_ref.shape)


def expert_first(at, pieces, gate_up, gain, early):
    units = gate_up.shape[1]
    return pl.pallas_call(
        first_kernel,
        in_specs=[SCALARS] + [WHOLE] * 6 + [pl.BlockSpec(memory_space=pl.ANY)],
        out_specs=[WHOLE] * 2,
        out_shape=[jax.ShapeDtypeStruct((256, units), F32), jax.ShapeDtypeStruct((256, HD), F32)],
        scratch_shapes=[pltpu.VMEM((256, HALF), BF)],
        compiler_params=pltpu.CompilerParams(vmem_limit_bytes=12 * MB),
        cost_estimate=pl.CostEstimate(flops=16000000000, bytes_accessed=9 * MB, transcendentals=0),
    )(at, *pieces, in_vmem(gate_up), gain, early)


def second_kernel(at_ref, p0, p1, p2, p3, w_ref, gain_ref, acc_ref, square_ref, inner_ref, x_ref, more_ref):
    units = inner_ref.shape[1]
    gathered(x_ref, (p0, p1, p2, p3), at_ref[2], False)
    square = square_ref[:, 0:1] + multiplied(x_ref, gain_ref, w_ref, 1 - at_ref[0], more_ref)
    scale = lax.rsqrt(square * (1.0 / D) + EPS)
    gate = (acc_ref[:, :units] + more_ref[:, :units]) * scale
    up = (acc_ref[:, units:] + more_ref[:, units:]) * scale
    inner_ref[...] = (gate / (1.0 + jnp.exp(-gate)) * up).astype(BF)


def expert_second(at, pieces, gate_up, gain, acc, square):
    units = gate_up.shape[1]
    return pl.pallas_call(
        second_kernel,
        in_specs=[SCALARS] + [WHOLE] * 8,
        out_specs=WHOLE,
        out_shape=jax.ShapeDtypeStruct((256, units // 2), BF),
        scratch_shapes=[pltpu.VMEM((256, HALF), BF), pltpu.VMEM((256, units), F32)],
        compiler_params=pltpu.CompilerParams(vmem_limit_bytes=12 * MB),
        cost_estimate=pl.CostEstimate(flops=1600000000, bytes_accessed=9 * MB, transcendentals=0),
    )(at, *pieces, in_vmem(gate_up), gain, acc, square)


def third_kernel(inner_ref, w_ref, out_ref):
    units = inner_ref.shape[1]
    width = HALF // 4
    for part in range(4):
        cols = slice(part * width, (part + 1) * width)
        out_ref[:, cols] = dot(inner_ref[...], w_ref[:units, cols])


def expert_third(inner, down):
    return pl.pallas_call(
        third_kernel,
        in_specs=[WHOLE] * 2,
        out_specs=WHOLE,
        out_shape=jax.ShapeDtypeStruct((inner.shape[0], HALF), F32),
        compiler_params=pltpu.CompilerParams(vmem_limit_bytes=12 * MB),
        cost_estimate=pl.CostEstimate(flops=8000000000, bytes_accessed=9 * MB, transcendentals=0),
    )(inner, in_vmem(down))


def fourth_kernel(at_ref, other_ref, w_ref, half_ref, *refs):
    outs, x_ref = refs[:-1], refs[-1]
    units = other_ref.shape[1]
    for a in range(4):
        for b in range(4):
            line, line_b = (4 * a + b) * 16, (4 * b + a) * 16
            x_ref[line : line + 16, :] = other_ref[line_b : line_b + 16, :]
    width = HALF // 4
    for part in range(4):
        cols = slice(part * width, (part + 1) * width)
        value = (half_ref[:, cols] + dot(x_ref[...], w_ref[units:, cols])).astype(BF)
        here = slice(part % 2 * width, (part % 2 + 1) * width)
        for a in range(4):
            for b in range(4):
                line = (4 * a + b) * 16
                outs[2 * a + part // 2][pl.ds(rolled(at_ref[1], b), 16), here] = value[line : line + 16]


def expert_fourth(at, other, down, half):
    return pl.pallas_call(
        fourth_kernel,
        in_specs=[SCALARS] + [WHOLE] * 3,
        out_specs=[WHOLE] * 8,
        out_shape=[jax.ShapeDtypeStruct((64, HALF // 2), BF)] * 8,
        scratch_shapes=[pltpu.VMEM(other.shape, BF)],
        compiler_params=pltpu.CompilerParams(vmem_limit_bytes=12 * MB),
        cost_estimate=pl.CostEstimate(flops=800000000, bytes_accessed=9 * MB, transcendentals=0),
    )(at, other, in_vmem(down), half)


def total_kernel(*refs):
    out_ref = refs[-1]
    width = HALF // 2
    for part in range(2):
        value = functools.reduce(jnp.add, [ref[...].astype(F32) for ref in refs[3 * part : 3 * part + 3]])
        for chip in range(16):
            out_ref[chip, :, part * width : (part + 1) * width] = value[4 * chip : 4 * chip + 4].astype(BF)


def total(first, second):
    return pl.pallas_call(
        total_kernel,
        in_specs=[WHOLE] * 6,
        out_specs=WHOLE,
        out_shape=jax.ShapeDtypeStruct((16, 4, HALF), BF),
        compiler_params=pltpu.CompilerParams(vmem_limit_bytes=8 * MB),
        cost_estimate=pl.CostEstimate(flops=1000000, bytes_accessed=2 * MB, transcendentals=0),
    )(*first, *second)


def mix_kernel(at_ref, got_ref, residual_ref, weights_ref, kept_ref, sent_ref):
    mixed = residual_ref[...]
    weights = weights_ref[...]
    for expert in range(4):
        value = functools.reduce(jnp.add, [got_ref[4 * line + expert].astype(F32) for line in range(4)])
        mixed = mixed + value * weights[:, expert : expert + 1]
    first = at_ref[0] == 0
    kept_ref[...] = jnp.where(first, mixed[0:2], mixed[2:4]).astype(BF)
    sent_ref[...] = jnp.where(first, mixed[2:4], mixed[0:2]).astype(BF)


def mix(at, got, residual, weights):
    return pl.pallas_call(
        mix_kernel,
        in_specs=[SCALARS] + [WHOLE] * 3,
        out_specs=[WHOLE] * 2,
        out_shape=[jax.ShapeDtypeStruct((2, HALF), BF)] * 2,
        compiler_params=pltpu.CompilerParams(vmem_limit_bytes=8 * MB),
        cost_estimate=pl.CostEstimate(flops=1000000, bytes_accessed=MB, transcendentals=0),
    )(at, got, residual, weights)


def swap(value):
    return lax.ppermute(value, "c", SWAP)


def local(
    queries,
    prefix_keys,
    prefix_values,
    suffix_keys,
    suffix_values,
    suffix_lengths,
    hidden_in,
    w_out,
    norm_gain,
    expert_ids,
    expert_weights,
    w_gate,
    w_up,
    w_down,
):
    c = lax.axis_index("c").astype(jnp.int32)
    z = lax.axis_index("z").astype(jnp.int32)
    y = lax.axis_index("y").astype(jnp.int32)
    chip = 4 * z + y
    at = jnp.stack([c, jnp.where(c == 0, z, y), jnp.where(c == 0, y, z), 4 * chip + 2 * c])

    def in_order(own, got, axis):
        return jnp.where(
            c == 0, jnp.concatenate([own, got], axis=axis), jnp.concatenate([got, own], axis=axis)
        )

    q = spread(queries)
    keys_b = swap(prefix_keys)
    values_b = swap(prefix_values)
    suffix_keys_b = swap(suffix_keys)
    suffix_values_b = swap(suffix_values)
    w_down_b = swap(w_down[0])
    q = lax.all_to_all(q, PLANE, split_axis=0, concat_axis=0, tiled=True).reshape(64, HALF)
    suffix = jnp.concatenate([suffix_keys, suffix_values], axis=-1).reshape(128, 2 * KV * HD)
    suffix_b = jnp.concatenate([suffix_keys_b, suffix_values_b], axis=-1).reshape(128, 2 * KV * HD)
    first = 4 * chip
    left = jnp.stack([suffix_lengths - (first + 2 * c), suffix_lengths - (first + 2 * (1 - c))], axis=1)
    left = jnp.tile(left.astype(jnp.int32), (4, 1))
    match = expert_ids[:, :, None] == jnp.arange(4, dtype=jnp.int32)[None, None, :]
    weights = jnp.sum(jnp.where(match, expert_weights[:, :, None], 0.0), axis=1)
    weights = in_order(weights, swap(weights), 0)
    gain = widen(norm_gain.reshape(1, D))
    early = (gain, at)
    parts = attend(q, prefix_keys, keys_b, prefix_values, values_b, suffix, suffix_b, left, early)
    parts = lax.all_to_all(parts, ("z", "y"), split_axis=0, concat_axis=0, tiled=True)
    other, attended = project_other(at, parts, w_out, hidden_in)
    other = swap(other)
    mine = project_mine(at, attended, w_out, hidden_in)
    summed = (mine.astype(F32) + other.astype(F32)).astype(BF).reshape(16, 4, HALF)
    summed = lax.all_to_all(summed, ("z", "y"), split_axis=0, concat_axis=0, tiled=True)
    residual, sent = settle(summed, w_down_b)
    wide = wide_groups()
    own = lax.all_to_all(
        sent, ALL, split_axis=0, concat_axis=0, tiled=True, axis_index_groups=wide
    ).reshape(64, HALF)
    pieces = [own] + [lax.ppermute(own, PLANE, line_shift(s)) for s in (1, 2, 3)]
    gate_up, down = fetch(at, own, w_gate[0], w_up[0], w_down[0], w_down_b)
    pieces_b = [swap(piece) for piece in pieces]
    acc, square = expert_first(at, pieces, gate_up, gain, weights)
    inner = expert_second(at, pieces_b, gate_up, gain, acc, square)
    other = swap(inner)
    out = expert_fourth(at, other, down, expert_third(inner, down))
    (a0, b0), (a1, b1), (a2, b2), (a3, b3) = [(out[2 * i], out[2 * i + 1]) for i in range(4)]
    ahead = lambda value: lax.ppermute(value, PLANE, line_shift(1))
    back = lambda value: lax.ppermute(value, PLANE, line_shift(3))
    plus = lambda first, second: (first.astype(F32) + second.astype(F32)).astype(BF)
    via_a, via_b = ahead(a2), back(b2)
    near_b, near_a = ahead(b3), back(a1)
    far_a, far_b = ahead(plus(a3, via_a)), back(plus(b1, via_b))
    out = total((a0, near_a, far_a), (b0, near_b, far_b))
    out = lax.all_to_all(
        out, ALL, split_axis=0, concat_axis=0, tiled=True, axis_index_groups=wide
    )
    kept, sent = mix(at, out, residual, weights)
    got = swap(sent)
    return in_order(kept, got, 1)


def solution(mesh):
    grid = Mesh(mesh.devices.reshape(4, 4, 4, 2), ALL)
    placed = (
        P(ALL, None),
        P(PLANE, None),
        P(PLANE, None),
        P("x", PLANE, None),
        P("x", PLANE, None),
        P("x"),
        P(ALL, None),
        P(PLANE, None),
        P(),
        P(ALL, None),
        P(ALL, None),
        P("x", None, PLANE),
        P("x", None, PLANE),
        P("x", PLANE, None),
    )
    return jax.shard_map(
        local, mesh=grid, in_specs=placed, out_specs=P(ALL, None), check_vma=False
    )
```

```python
import functools

import jax
import jax.numpy as jnp
from jax import lax
from jax.experimental import pallas as pl
from jax.experimental.pallas import tpu as pltpu
from jax.sharding import Mesh, PartitionSpec as P

HEADS = 64
KV = 8
HD = 128
D = 8192
HALF = D // 2
EPS = 1e-05
NEG = -1e30
LOG2E = 1.4426950408889634
SCALE = LOG2E / HD**0.5
BF = jnp.bfloat16
F32 = jnp.float32
ALL = ("x", "z", "y", "c")
PLANE = ("z", "y", "c")
SWAP = [(0, 1), (1, 0)]
MB = 1 << 20
WHOLE = pl.BlockSpec(memory_space=pltpu.VMEM)
SCALARS = pl.BlockSpec(memory_space=pltpu.SMEM)


def device(x, z, y, c):
    return ((x * 4 + z) * 4 + y) * 2 + c


def wide_groups():
    four = range(4)
    zeros = [[device(x, z, y, 0) for z in four for x in four] for y in four]
    return zeros + [[device(x, z, y, 1) for y in four for x in four] for z in four]


def line_shift(step):
    pairs = []
    for z in range(4):
        for y in range(4):
            pairs.append(((z * 4 + y) * 2, (z * 4 + (y + step) % 4) * 2))
            pairs.append(((z * 4 + y) * 2 + 1, (((z + step) % 4) * 4 + y) * 2 + 1))
    return pairs


def dot(a, b):
    return jnp.dot(a, b, preferred_element_type=F32)


def dot_t(a, b):
    return lax.dot_general(a, b, (((1,), (1,)), ((), ())), preferred_element_type=F32)


def fetch_kernel(at_ref, after_ref, wg_ref, wu_ref, wd_ref, wdb_ref, gate_up_ref, down_ref, sems):
    units = wg_ref.shape[1]
    pairs = []
    for part in range(4):
        rows = pl.ds(part * D // 4, D // 4)
        pairs.append((wg_ref.at[rows], gate_up_ref.at[rows, pl.ds(0, units)]))
        pairs.append((wu_ref.at[rows], gate_up_ref.at[rows, pl.ds(units, units)]))
    columns = pl.ds(pl.multiple_of(at_ref[0] * HALF, HALF), HALF)
    for part in range(2):
        rows = pl.ds(part * units // 2, units // 2)
        pairs.append((wd_ref.at[rows, columns], down_ref.at[rows]))
        rows_b = pl.ds(units + part * units // 2, units // 2)
        pairs.append((wdb_ref.at[rows, columns], down_ref.at[rows_b]))
    copies = [pltpu.make_async_copy(src, dst, sems.at[i]) for i, (src, dst) in enumerate(pairs)]
    for copy in copies:
        copy.start()
    for copy in copies:
        copy.wait()


def fetch(at, after, w_gate, w_up, w_down, w_down_b):
    units = w_gate.shape[1]
    return pl.pallas_call(
        fetch_kernel,
        in_specs=[SCALARS] + [pl.BlockSpec(memory_space=pl.ANY)] * 5,
        out_specs=[WHOLE] * 2,
        out_shape=[pltpu.VMEM((D, 2 * units), BF), pltpu.VMEM((2 * units, HALF), BF)],
        scratch_shapes=[pltpu.SemaphoreType.DMA((12,))],
        compiler_params=pltpu.CompilerParams(vmem_limit_bytes=4 * MB),
        cost_estimate=pl.CostEstimate(flops=0, bytes_accessed=22 * MB, transcendentals=0),
    )(at, after, in_hbm(w_gate), in_hbm(w_up), in_hbm(w_down), in_hbm(w_down_b))


def in_vmem(array):
    return pltpu.with_memory_space_constraint(array, pltpu.VMEM)


def in_hbm(array):
    return pltpu.with_memory_space_constraint(array, pltpu.HBM)


def spread_kernel(q_ref, out_ref):
    for half in range(2):
        value = jnp.concatenate(
            [q_ref[:, (2 * k + half) * 2 * HD : (2 * k + half + 1) * 2 * HD] for k in range(16)], axis=1
        )
        for chip in range(16):
            out_ref[2 * chip + half] = value


def spread(queries):
    return pl.pallas_call(
        spread_kernel,
        grid=(1,),
        in_specs=[pl.BlockSpec((2, D), lambda i: (0, 0))],
        out_specs=pl.BlockSpec((32, 2, HALF), lambda i: (0, 0, 0)),
        out_shape=jax.ShapeDtypeStruct((32, 2, HALF), BF),
        compiler_params=pltpu.CompilerParams(vmem_limit_bytes=4 * MB),
        cost_estimate=pl.CostEstimate(flops=0, bytes_accessed=MB, transcendentals=0),
    )(in_hbm(queries))


def widen_kernel(gain_ref, out_ref):
    out_ref[...] = gain_ref[...].astype(F32)


def widen(gain):
    whole = pl.BlockSpec((1, D), lambda i: (0, 0))
    return pl.pallas_call(
        widen_kernel,
        grid=(1,),
        in_specs=[whole],
        out_specs=whole,
        out_shape=jax.ShapeDtypeStruct((1, D), F32),
        compiler_params=pltpu.CompilerParams(vmem_limit_bytes=4 * MB),
        cost_estimate=pl.CostEstimate(flops=20000000000, bytes_accessed=MB, transcendentals=0),
    )(gain)


def store_part(out_ref, first, acc, top, total):
    rows = 64
    size = (4 * rows, 4 * rows)
    eye = lax.broadcasted_iota(jnp.int32, size, 0) == lax.broadcasted_iota(jnp.int32, size, 1)
    top_row = jnp.sum(jnp.where(eye, top, 0.0), axis=0, keepdims=True)
    total_row = jnp.sum(jnp.where(eye, total, 0.0), axis=0, keepdims=True)
    total_high = total_row.astype(BF).astype(F32)
    total_low = total_row - total_high
    line = lax.broadcasted_iota(jnp.int32, (8, 4 * rows), 0)
    for k in range(2):
        for j in range(2):
            g = 2 * k + j
            out_ref[first + k, 0:rows, j * HD : (j + 1) * HD] = acc[g * rows : (g + 1) * rows].astype(BF)
        part = slice(k * 2 * rows, (k + 1) * 2 * rows)
        high = jnp.concatenate([top_row[:, part], total_high[:, part]], axis=1)
        low = jnp.concatenate([top_row[:, part], total_low[:, part]], axis=1)
        tail = jnp.where(line == 0, high, jnp.where(line == 1, low, 0.0))
        out_ref[first + k, rows : rows + 8, :] = tail.astype(BF)


def attend_kernel(q_ref, ka_ref, kb_ref, va_ref, vb_ref, sa_ref, sb_ref, left_ref, *refs):
    out_ref = refs[-1]
    rows = 64
    row = lax.broadcasted_iota(jnp.int32, (4 * rows, 4 * rows), 0)
    col = lax.broadcasted_iota(jnp.int32, (4 * rows, 4 * rows), 1)
    left = left_ref[...]
    live = (row % rows == col % (2 * rows) // 2) & (
        col % 2 < jnp.where(col < 2 * rows, left[:, 0:1], left[:, 1:2])
    )
    for h in range(KV):
        at = slice(h * HD, (h + 1) * HD)
        at_v = slice((KV + h) * HD, (KV + h + 1) * HD)
        q = jnp.concatenate(
            [q_ref[:, (4 * h + g) * HD : (4 * h + g + 1) * HD] for g in range(4)], axis=0
        )
        suffix_k = jnp.concatenate([sa_ref[:, at], sb_ref[:, at]], axis=0)
        suffix_v = jnp.concatenate([sa_ref[:, at_v], sb_ref[:, at_v]], axis=0)
        scores = [
            dot_t(q, ka_ref[:, at]),
            dot_t(q, kb_ref[:, at]),
            jnp.where(live, dot_t(q, suffix_k), NEG),
        ]
        top = functools.reduce(jnp.maximum, [jnp.max(s, axis=1, keepdims=True) for s in scores])
        top = (top * SCALE).astype(BF).astype(F32)
        total, acc = 0.0, 0.0
        for s, v in zip(scores, (va_ref[:, at], vb_ref[:, at], suffix_v)):
            prob = jnp.exp2(s * SCALE - top)
            total = total + jnp.sum(prob, axis=1, keepdims=True)
            acc = acc + dot(prob.astype(BF), v)
        store_part(out_ref, 2 * h, acc, top, total)


def attend(q, ka, kb, va, vb, sa, sb, left, early):
    arrays = (q, ka, kb, va, vb, sa, sb, left)
    return pl.pallas_call(
        attend_kernel,
        grid=(1,),
        in_specs=[pl.BlockSpec(a.shape, lambda i: (0, 0)) for a in arrays]
        + [pl.BlockSpec(memory_space=pl.ANY)] * len(early),
        out_specs=pl.BlockSpec((16, 72, 2 * HD), lambda i: (0, 0, 0)),
        out_shape=jax.ShapeDtypeStruct((16, 72, 2 * HD), BF),
        compiler_params=pltpu.CompilerParams(vmem_limit_bytes=24 * MB),
        cost_estimate=pl.CostEstimate(flops=1400000000, bytes_accessed=6 * MB, transcendentals=2700000),
    )(q, in_hbm(ka), kb, in_hbm(va), vb, sa, sb, left, *early)


def half_product(attended, w_ref, half, hidden_ref, first, out_ref):
    width = HALF // 4
    line = lax.broadcasted_iota(jnp.int32, (out_ref.shape[0], 1), 0)
    picks = [(line == first + i).astype(F32) for i in range(2)]
    for part in range(4):
        cols = pl.ds(pl.multiple_of(half * HALF + part * width, width), width)
        value = dot(attended, w_ref[:, cols])
        hidden = hidden_ref[:, cols].astype(F32)
        value = value + picks[0] * hidden[0:1] + picks[1] * hidden[1:2]
        out_ref[:, part * width : (part + 1) * width] = value.astype(BF)


def project_kernel(at_ref, got_ref, w_ref, hidden_ref, out_ref, att_ref):
    rows = 64
    tops = [got_ref[s, rows : rows + 1, 0 : 2 * rows].astype(F32) for s in range(16)]
    sums = [
        got_ref[s, rows : rows + 1, 2 * rows :].astype(F32)
        + got_ref[s, rows + 1 : rows + 2, 2 * rows :].astype(F32)
        for s in range(16)
    ]
    top = functools.reduce(jnp.maximum, tops)
    factors = [jnp.exp2(t - top) for t in tops]
    total = functools.reduce(jnp.add, [f * s for f, s in zip(factors, sums)])
    lane = lax.broadcasted_iota(jnp.int32, (rows, 2 * rows), 1)
    line = lax.broadcasted_iota(jnp.int32, (rows, 2 * rows), 0)
    for j in range(2):
        here = lane == line + j * rows
        acc = jnp.zeros((rows, HD), F32)
        for s in range(16):
            share = jnp.sum(jnp.where(here, factors[s] / total, 0.0), axis=1, keepdims=True)
            acc = acc + got_ref[s, 0:rows, j * HD : (j + 1) * HD].astype(F32) * share
        att_ref[:, j * HD : (j + 1) * HD] = acc.astype(BF)
    half_product(att_ref[...], w_ref, 1 - at_ref[0], hidden_ref, at_ref[3], out_ref)


def project_other(at, got, w_out, hidden):
    return pl.pallas_call(
        project_kernel,
        in_specs=[SCALARS] + [WHOLE] * 3,
        out_specs=[WHOLE] * 2,
        out_shape=[jax.ShapeDtypeStruct((64, HALF), BF), jax.ShapeDtypeStruct((64, 256), BF)],
        compiler_params=pltpu.CompilerParams(vmem_limit_bytes=16 * MB),
        cost_estimate=pl.CostEstimate(flops=140000000, bytes_accessed=3 * MB, transcendentals=0),
    )(at, got, in_vmem(w_out), in_vmem(hidden))


def project_mine_kernel(at_ref, att_ref, w_ref, hidden_ref, out_ref):
    half_product(att_ref[...], w_ref, at_ref[0], hidden_ref, at_ref[3], out_ref)


def project_mine(at, attended, w_out, hidden):
    return pl.pallas_call(
        project_mine_kernel,
        in_specs=[SCALARS] + [WHOLE] * 3,
        out_specs=WHOLE,
        out_shape=jax.ShapeDtypeStruct((64, HALF), BF),
        compiler_params=pltpu.CompilerParams(vmem_limit_bytes=16 * MB),
        cost_estimate=pl.CostEstimate(flops=140000000, bytes_accessed=3 * MB, transcendentals=0),
    )(at, attended, in_vmem(w_out), in_vmem(hidden))


def settle_kernel(got_ref, early_ref, residual_ref, sent_ref):
    residual = functools.reduce(jnp.add, [got_ref[i].astype(F32) for i in range(16)])
    residual_ref[...] = residual
    for i in range(16):
        sent_ref[i] = residual.astype(BF)


def settle(got, early):
    return pl.pallas_call(
        settle_kernel,
        in_specs=[WHOLE, pl.BlockSpec(memory_space=pl.ANY)],
        out_specs=[WHOLE] * 2,
        out_shape=[jax.ShapeDtypeStruct((4, HALF), F32), jax.ShapeDtypeStruct((16, 4, HALF), BF)],
        compiler_params=pltpu.CompilerParams(vmem_limit_bytes=8 * MB),
        cost_estimate=pl.CostEstimate(flops=1000000, bytes_accessed=MB, transcendentals=0),
    )(got, in_hbm(early))


def rolled(place, back):
    return pl.multiple_of(((place + 4 - back) & 3) * 16, 16)


def gathered(x_ref, pieces, place, own):
    for a in range(4):
        for b in range(4):
            piece, back = (a, b) if own else (b, a)
            line = (4 * a + b) * 16
            x_ref[line : line + 16, :] = pieces[piece][pl.ds(rolled(place, back), 16), :]


def multiplied(x_ref, gain_ref, w_ref, half, acc_ref):
    width = HALF // 4
    square = 0.0
    for part in range(4):
        rows = pl.ds(pl.multiple_of(half * HALF + part * width, width), width)
        x = x_ref[:, part * width : (part + 1) * width].astype(F32)
        square = square + jnp.sum(x * x, axis=1, keepdims=True)
        value = dot((x * gain_ref[:, rows]).astype(BF), w_ref[rows, :])
        if part == 0:
            acc_ref[...] = value
        else:
            acc_ref[...] += value
    return square


def first_kernel(at_ref, p0, p1, p2, p3, w_ref, gain_ref, early_ref, acc_ref, square_ref, x_ref):
    gathered(x_ref, (p0, p1, p2, p3), at_ref[1], True)
    square = multiplied(x_ref, gain_ref, w_ref, at_ref[0], acc_ref)
    square_ref[...] = jnp.broadcast_to(square, square_ref.shape)


def expert_first(at, pieces, gate_up, gain, early):
    units = gate_up.shape[1]
    return pl.pallas_call(
        first_kernel,
        in_specs=[SCALARS] + [WHOLE] * 6 + [pl.BlockSpec(memory_space=pl.ANY)],
        out_specs=[WHOLE] * 2,
        out_shape=[jax.ShapeDtypeStruct((256, units), F32), jax.ShapeDtypeStruct((256, HD), F32)],
        scratch_shapes=[pltpu.VMEM((256, HALF), BF)],
        compiler_params=pltpu.CompilerParams(vmem_limit_bytes=12 * MB),
        cost_estimate=pl.CostEstimate(flops=16000000000, bytes_accessed=9 * MB, transcendentals=0),
    )(at, *pieces, in_vmem(gate_up), gain, early)


def second_kernel(at_ref, p0, p1, p2, p3, w_ref, gain_ref, acc_ref, square_ref, inner_ref, x_ref, more_ref):
    units = inner_ref.shape[1]
    gathered(x_ref, (p0, p1, p2, p3), at_ref[2], False)
    square = square_ref[:, 0:1] + multiplied(x_ref, gain_ref, w_ref, 1 - at_ref[0], more_ref)
    scale = lax.rsqrt(square * (1.0 / D) + EPS)
    gate = (acc_ref[:, :units] + more_ref[:, :units]) * scale
    up = (acc_ref[:, units:] + more_ref[:, units:]) * scale
    inner_ref[...] = (gate / (1.0 + jnp.exp(-gate)) * up).astype(BF)


def expert_second(at, pieces, gate_up, gain, acc, square):
    units = gate_up.shape[1]
    return pl.pallas_call(
        second_kernel,
        in_specs=[SCALARS] + [WHOLE] * 8,
        out_specs=WHOLE,
        out_shape=jax.ShapeDtypeStruct((256, units // 2), BF),
        scratch_shapes=[pltpu.VMEM((256, HALF), BF), pltpu.VMEM((256, units), F32)],
        compiler_params=pltpu.CompilerParams(vmem_limit_bytes=12 * MB),
        cost_estimate=pl.CostEstimate(flops=1600000000, bytes_accessed=9 * MB, transcendentals=0),
    )(at, *pieces, in_vmem(gate_up), gain, acc, square)


def third_kernel(inner_ref, w_ref, out_ref):
    units = inner_ref.shape[1]
    width = HALF // 4
    for part in range(4):
        cols = slice(part * width, (part + 1) * width)
        out_ref[:, cols] = dot(inner_ref[...], w_ref[:units, cols])


def expert_third(inner, down):
    return pl.pallas_call(
        third_kernel,
        in_specs=[WHOLE] * 2,
        out_specs=WHOLE,
        out_shape=jax.ShapeDtypeStruct((inner.shape[0], HALF), F32),
        compiler_params=pltpu.CompilerParams(vmem_limit_bytes=12 * MB),
        cost_estimate=pl.CostEstimate(flops=8000000000, bytes_accessed=9 * MB, transcendentals=0),
    )(inner, in_vmem(down))


def fourth_kernel(at_ref, other_ref, w_ref, half_ref, *refs):
    outs, x_ref = refs[:-1], refs[-1]
    units = other_ref.shape[1]
    for a in range(4):
        for b in range(4):
            line, line_b = (4 * a + b) * 16, (4 * b + a) * 16
            x_ref[line : line + 16, :] = other_ref[line_b : line_b + 16, :]
    width = HALF // 4
    for part in range(4):
        cols = slice(part * width, (part + 1) * width)
        value = (half_ref[:, cols] + dot(x_ref[...], w_ref[units:, cols])).astype(BF)
        here = slice(part % 2 * width, (part % 2 + 1) * width)
        for a in range(4):
            for b in range(4):
                line = (4 * a + b) * 16
                outs[2 * a + part // 2][pl.ds(rolled(at_ref[1], b), 16), here] = value[line : line + 16]


def expert_fourth(at, other, down, half):
    return pl.pallas_call(
        fourth_kernel,
        in_specs=[SCALARS] + [WHOLE] * 3,
        out_specs=[WHOLE] * 8,
        out_shape=[jax.ShapeDtypeStruct((64, HALF // 2), BF)] * 8,
        scratch_shapes=[pltpu.VMEM(other.shape, BF)],
        compiler_params=pltpu.CompilerParams(vmem_limit_bytes=12 * MB),
        cost_estimate=pl.CostEstimate(flops=800000000, bytes_accessed=9 * MB, transcendentals=0),
    )(at, other, in_vmem(down), half)


def total_kernel(count, *refs):
    out_ref = refs[-1]
    width = HALF // 2
    for part, terms in enumerate((refs[:count], refs[count:-1])):
        value = functools.reduce(jnp.add, [ref[...].astype(F32) for ref in terms])
        for chip in range(16):
            out_ref[chip, :, part * width : (part + 1) * width] = value[4 * chip : 4 * chip + 4].astype(BF)


def total(first, second):
    return pl.pallas_call(
        functools.partial(total_kernel, len(first)),
        in_specs=[WHOLE] * (len(first) + len(second)),
        out_specs=WHOLE,
        out_shape=jax.ShapeDtypeStruct((16, 4, HALF), BF),
        compiler_params=pltpu.CompilerParams(vmem_limit_bytes=8 * MB),
        cost_estimate=pl.CostEstimate(flops=1000000, bytes_accessed=2 * MB, transcendentals=0),
    )(*first, *second)


def mix_kernel(at_ref, got_ref, residual_ref, weights_ref, kept_ref, sent_ref):
    mixed = residual_ref[...]
    weights = weights_ref[...]
    for expert in range(4):
        value = functools.reduce(jnp.add, [got_ref[4 * line + expert].astype(F32) for line in range(4)])
        mixed = mixed + value * weights[:, expert : expert + 1]
    first = at_ref[0] == 0
    kept_ref[...] = jnp.where(first, mixed[0:2], mixed[2:4]).astype(BF)
    sent_ref[...] = jnp.where(first, mixed[2:4], mixed[0:2]).astype(BF)


def mix(at, got, residual, weights):
    return pl.pallas_call(
        mix_kernel,
        in_specs=[SCALARS] + [WHOLE] * 3,
        out_specs=[WHOLE] * 2,
        out_shape=[jax.ShapeDtypeStruct((2, HALF), BF)] * 2,
        compiler_params=pltpu.CompilerParams(vmem_limit_bytes=8 * MB),
        cost_estimate=pl.CostEstimate(flops=1000000, bytes_accessed=MB, transcendentals=0),
    )(at, got, residual, weights)


def swap(value):
    return lax.ppermute(value, "c", SWAP)


def local(
    queries,
    prefix_keys,
    prefix_values,
    suffix_keys,
    suffix_values,
    suffix_lengths,
    hidden_in,
    w_out,
    norm_gain,
    expert_ids,
    expert_weights,
    w_gate,
    w_up,
    w_down,
):
    c = lax.axis_index("c").astype(jnp.int32)
    z = lax.axis_index("z").astype(jnp.int32)
    y = lax.axis_index("y").astype(jnp.int32)
    chip = 4 * z + y
    at = jnp.stack([c, jnp.where(c == 0, z, y), jnp.where(c == 0, y, z), 4 * chip + 2 * c])

    def in_order(own, got, axis):
        return jnp.where(
            c == 0, jnp.concatenate([own, got], axis=axis), jnp.concatenate([got, own], axis=axis)
        )

    q = spread(queries)
    keys_b = swap(prefix_keys)
    values_b = swap(prefix_values)
    suffix_keys_b = swap(suffix_keys)
    suffix_values_b = swap(suffix_values)
    w_down_b = swap(w_down[0])
    q = lax.all_to_all(q, PLANE, split_axis=0, concat_axis=0, tiled=True).reshape(64, HALF)
    suffix = jnp.concatenate([suffix_keys, suffix_values], axis=-1).reshape(128, 2 * KV * HD)
    suffix_b = jnp.concatenate([suffix_keys_b, suffix_values_b], axis=-1).reshape(128, 2 * KV * HD)
    first = 4 * chip
    left = jnp.stack([suffix_lengths - (first + 2 * c), suffix_lengths - (first + 2 * (1 - c))], axis=1)
    left = jnp.tile(left.astype(jnp.int32), (4, 1))
    match = expert_ids[:, :, None] == jnp.arange(4, dtype=jnp.int32)[None, None, :]
    weights = jnp.sum(jnp.where(match, expert_weights[:, :, None], 0.0), axis=1)
    weights = in_order(weights, swap(weights), 0)
    gain = widen(norm_gain.reshape(1, D))
    early = (gain, at)
    parts = attend(q, prefix_keys, keys_b, prefix_values, values_b, suffix, suffix_b, left, early)
    parts = lax.all_to_all(parts, ("z", "y"), split_axis=0, concat_axis=0, tiled=True)
    other, attended = project_other(at, parts, w_out, hidden_in)
    other = swap(other)
    mine = project_mine(at, attended, w_out, hidden_in)
    summed = (mine.astype(F32) + other.astype(F32)).astype(BF).reshape(16, 4, HALF)
    summed = lax.all_to_all(summed, ("z", "y"), split_axis=0, concat_axis=0, tiled=True)
    residual, sent = settle(summed, w_down_b)
    wide = wide_groups()
    own = lax.all_to_all(
        sent, ALL, split_axis=0, concat_axis=0, tiled=True, axis_index_groups=wide
    ).reshape(64, HALF)
    pieces = [own] + [lax.ppermute(own, PLANE, line_shift(s)) for s in (1, 2, 3)]
    gate_up, down = fetch(at, own, w_gate[0], w_up[0], w_down[0], w_down_b)
    pieces_b = [swap(piece) for piece in pieces]
    acc, square = expert_first(at, pieces, gate_up, gain, weights)
    inner = expert_second(at, pieces_b, gate_up, gain, acc, square)
    other = swap(inner)
    out = expert_fourth(at, other, down, expert_third(inner, down))
    (a0, b0), (a1, b1), (a2, b2), (a3, b3) = [(out[2 * i], out[2 * i + 1]) for i in range(4)]
    ahead = lambda value: lax.ppermute(value, PLANE, line_shift(1))
    back = lambda value: lax.ppermute(value, PLANE, line_shift(3))
    plus = lambda first, second: (first.astype(F32) + second.astype(F32)).astype(BF)
    via_b = back(b2)
    two_a = lax.ppermute(a2, PLANE, line_shift(2))
    three_a, three_b = ahead(a3), ahead(b3)
    one_a = back(a1)
    one_b = back(plus(b1, via_b))
    out = total((a0, one_a, three_a, two_a), (b0, three_b, one_b))
    out = lax.all_to_all(
        out, ALL, split_axis=0, concat_axis=0, tiled=True, axis_index_groups=wide
    )
    kept, sent = mix(at, out, residual, weights)
    got = swap(sent)
    return in_order(kept, got, 1)


def solution(mesh):
    grid = Mesh(mesh.devices.reshape(4, 4, 4, 2), ALL)
    placed = (
        P(ALL, None),
        P(PLANE, None),
        P(PLANE, None),
        P("x", PLANE, None),
        P("x", PLANE, None),
        P("x"),
        P(ALL, None),
        P(PLANE, None),
        P(),
        P(ALL, None),
        P(ALL, None),
        P("x", None, PLANE),
        P("x", None, PLANE),
        P("x", PLANE, None),
    )
    return jax.shard_map(
        local, mesh=grid, in_specs=placed, out_specs=P(ALL, None), check_vma=False
    )
```
